128 devices in a mesh: seq: 16 (over y, x_lo, core), tp: 8 (over x_hi, z).
Axes of the slice: x: 4 (x_hi: 2, x_lo: 2; x = x_hi * 2 + x_lo), y: 4, z: 4, core: 2. Of those that a mesh axis runs over, the one named last changes fastest.
Arguments:
- queries: bfloat16 [2, 4096, 3072], P(None, 'seq', 'tp'), may hold values from -8 to 8
- keys: bfloat16 [2, 4096, 3072], P(None, 'seq', 'tp'), may hold values from -8 to 8
- values: bfloat16 [2, 4096, 3072], P(None, 'seq', 'tp'), may hold values from -6 to 6
- block_order: int32 [256], P('seq'), may hold values from 0 to 255, each once
- out_weight: bfloat16 [3072, 5120], P('tp'), may hold values from -0.109375 to 0.109375
- out_grad: bfloat16 [2, 4096, 5120], P(None, 'seq', 'tp'), may hold values from -6 to 6
Outputs:
- mixed: bfloat16 [2, 4096, 5120], P(None, 'seq', 'tp')
- query_grad: bfloat16 [2, 4096, 3072], P(None, 'seq', 'tp')
- key_grad: bfloat16 [2, 4096, 3072], P(None, 'seq', 'tp')
- value_grad: bfloat16 [2, 4096, 3072], P(None, 'seq', 'tp')
- weight_grad: float32 [3072, 5120], P('tp', 'seq')
The draws below stay inside these ranges and needn't reach their ends.
Inputs may be any that keep to these rules, and one draw needn't show every extreme that they name: `block_order`: a permutation of the block positions.
All inputs are finite; a program needn't handle non-finite values.
Results may differ from the reference program's by a relative error of at most 0.029.
Values may be sent and summed in bfloat16 or wider, within the bound.
A program may use at most 128 MiB of HBM per device.

```python
import math
import jax
import jax.numpy as jnp
from jax import lax

D = 5120
HEADS = 24
HEAD_SIZE = 128
BLOCK = 16
CLEAN_TOKENS = 4096
BLOCKS = 256
INNER = 3072
INNER_DEV = 384
N_TP = 8


def draw_queries(key, part):
    key = jax.random.fold_in(key, 7)
    drawn_values = jnp.clip(jax.random.normal(key, (2, CLEAN_TOKENS, INNER), jnp.float32), -6.0, 6.0)
    return drawn_values.astype(jnp.bfloat16)


def draw_keys(key, part):
    key = jax.random.fold_in(key, 13)
    drawn_values = jnp.clip(jax.random.normal(key, (2, CLEAN_TOKENS, INNER), jnp.float32), -6.0, 6.0)
    return drawn_values.astype(jnp.bfloat16)


def with_spikes(drawn, key, source, target, parts, factor):
    def block_of(axis_at):
        return (jnp.arange(drawn.shape[axis_at]) // (drawn.shape[axis_at] // parts)).reshape((-1,) + (1,) * (drawn.ndim - 1 - axis_at))

    near = jax.random.permutation(key, parts)[block_of(target)]
    far = (block_of(target) + parts // 2) % parts
    return jnp.where((block_of(source) == near) | (block_of(source) == far), factor * drawn, drawn)


def block_levels(key, dims, cuts, low, high):
    def one(axis_at, shards_of):
        heights = jax.random.uniform(jax.random.fold_in(jax.random.fold_in(key, 6), axis_at), (shards_of,), jnp.float32, low / len(cuts), high / len(cuts))
        return jnp.repeat(jnp.exp(heights), dims[axis_at] // shards_of).reshape((-1,) + (1,) * (len(dims) - axis_at - 1))

    gain = one(*cuts[0])
    for cut in cuts[1:]:
        gain = gain * one(*cut)
    return gain


def normal_values(stream_key, dims, scale, most, cuts=(), kind=jnp.bfloat16):
    factor_of = block_levels(stream_key, dims, cuts, -0.22, 0.18) if cuts else 1.0
    drawn = jax.random.normal(stream_key, dims, jnp.float32) * scale * factor_of
    return jnp.minimum(jnp.maximum(drawn, -most), most).astype(kind)


def heavy_noise(stream_key, dims, scale, bound, split, heavy, kind=jnp.bfloat16):
    values = scale * jax.random.normal(stream_key, dims, jnp.float32)
    if split:
        values = values * block_levels(stream_key, dims, split, -0.22, 0.18)
    return jnp.clip(with_spikes(values, jax.random.fold_in(stream_key, 3), *heavy), -bound, bound).astype(kind)


def setup_inputs(seed: int = 0) -> dict:
    splits = jax.random.split(jax.random.key(seed), 7)
    queries = draw_queries(jax.random.fold_in(splits[6], 71), 0)
    keys = draw_keys(jax.random.fold_in(splits[6], 71), 0)
    values = normal_values(splits[2], (2, CLEAN_TOKENS, INNER), 1.0, 6.0, ((1, 16), (2, 8)))
    block_order = jax.random.permutation(splits[3], BLOCKS).astype(jnp.int32)
    out_weight = normal_values(splits[4], (INNER, D), INNER ** -0.5, 0.109375, ((0, 8),))
    out_grad = heavy_noise(splits[5], (2, CLEAN_TOKENS, D), 1.0, 6.0, ((1, 16), (2, 8)), (1, 2, 16, 2.0))
    return {"queries": queries, "keys": keys, "values": values, "block_order": block_order, "out_weight": out_weight, "out_grad": out_grad}


masked_score = -1e+30

def rounded_result(array):
    return lax.optimization_barrier(array.astype(jnp.bfloat16)).astype(jnp.float32)

def visibility(block_order):
    position = jnp.repeat(block_order, BLOCK)
    offset = jnp.arange(CLEAN_TOKENS, dtype=jnp.int32) % BLOCK
    earlier = position[None, :] < position[:, None]
    causal = earlier | (position[None, :] == position[:, None]) & (offset[None, :] <= offset[:, None])
    return (causal, earlier)

def block_layout(array):
    return array.reshape(BLOCKS, BLOCK, HEAD_SIZE).astype(jnp.float32)

def head_forward(query_couple, key_couple, value_couple, causal, earlier):
    scale_factor = 1.0 / math.sqrt(HEAD_SIZE)
    clean_scores = jnp.where(causal, jnp.dot(query_couple[0], key_couple[0].T, preferred_element_type=jnp.float32) * scale_factor, masked_score)
    noisy_scores = jnp.where(earlier, jnp.dot(query_couple[1], key_couple[0].T, preferred_element_type=jnp.float32) * scale_factor, masked_score)
    self_block_scores = jnp.einsum('rgi,rsi->rgs', block_layout(query_couple[1]), block_layout(key_couple[1])) * scale_factor
    clean_top = lax.optimization_barrier(jnp.max(clean_scores, axis=1))
    noisy_top = jnp.maximum(lax.optimization_barrier(jnp.max(noisy_scores, axis=1)), lax.optimization_barrier(jnp.max(self_block_scores, axis=2)).reshape(CLEAN_TOKENS))
    clean_exp = jnp.where(causal, jnp.exp(clean_scores - clean_top[:, None]), 0.0)
    noisy_exp = jnp.where(earlier, jnp.exp(noisy_scores - noisy_top[:, None]), 0.0)
    self_exponent = jnp.exp(self_block_scores - noisy_top.reshape(BLOCKS, BLOCK, 1))
    clean_total = lax.optimization_barrier(jnp.sum(clean_exp, axis=1))
    noisy_total = lax.optimization_barrier(jnp.sum(noisy_exp, axis=1)) + lax.optimization_barrier(jnp.sum(self_exponent, axis=2)).reshape(CLEAN_TOKENS)
    clean_acc = jnp.dot(clean_exp.astype(jnp.bfloat16), value_couple[0], preferred_element_type=jnp.float32)
    self_accumulator = jnp.einsum('ifg,igr->ifr', rounded_result(self_exponent), block_layout(value_couple[1])).reshape(CLEAN_TOKENS, HEAD_SIZE)
    noisy_acc = jnp.dot(noisy_exp.astype(jnp.bfloat16), value_couple[0], preferred_element_type=jnp.float32) + self_accumulator
    attention_pair = jnp.stack([clean_acc / clean_total[:, None], noisy_acc / noisy_total[:, None]]).astype(jnp.bfloat16)
    log_total = jnp.stack([clean_top + jnp.log(clean_total), noisy_top + jnp.log(noisy_total)])
    return (attention_pair, log_total)

def head_backward(query_couple, key_couple, value_couple, attention_pair, grad_pair, log_total, causal, earlier):
    scale_factor = 1.0 / math.sqrt(HEAD_SIZE)
    row_delta = lax.optimization_barrier(jnp.sum(grad_pair.astype(jnp.float32) * attention_pair.astype(jnp.float32), axis=2))

    def far_terms(query_one, grad_one, total_one, delta_one, visible):
        scores = jnp.where(visible, jnp.dot(query_one, key_couple[0].T, preferred_element_type=jnp.float32) * scale_factor, masked_score)
        prob_weights = jnp.where(visible, jnp.exp(scores - total_one[:, None]), 0.0)
        value_term = jnp.dot(prob_weights.astype(jnp.bfloat16).T, grad_one, preferred_element_type=jnp.float32)
        prob_grad = jnp.dot(grad_one, value_couple[0].T, preferred_element_type=jnp.float32)
        score_grad = (prob_weights * (prob_grad - delta_one[:, None])).astype(jnp.bfloat16)
        query_term = jnp.dot(score_grad, key_couple[0], preferred_element_type=jnp.float32) * scale_factor
        key_term = jnp.dot(score_grad.T, query_one, preferred_element_type=jnp.float32) * scale_factor
        return (query_term, key_term, value_term)
    clean_query, clean_key, clean_value = far_terms(query_couple[0], grad_pair[0], log_total[0], row_delta[0], causal)
    noisy_query, noisy_key, noisy_value = far_terms(query_couple[1], grad_pair[1], log_total[1], row_delta[1], earlier)
    self_block_queries = block_layout(query_couple[1])
    self_block_keys = block_layout(key_couple[1])
    self_block_values = block_layout(value_couple[1])
    self_gradients = block_layout(grad_pair[1])
    self_block_scores = jnp.einsum('rgi,rsi->rgs', self_block_queries, self_block_keys) * scale_factor
    self_probabilities = jnp.exp(self_block_scores - log_total[1].reshape(BLOCKS, BLOCK, 1))
    self_value_contribution = jnp.einsum('urs,urh->ush', rounded_result(self_probabilities), self_gradients).reshape(CLEAN_TOKENS, HEAD_SIZE)
    self_probability_gradient = jnp.einsum('rgi,rsi->rgs', self_gradients, self_block_values)
    self_score_gradient = rounded_result(self_probabilities * (self_probability_gradient - row_delta[1].reshape(BLOCKS, BLOCK, 1)))
    self_query_contribution = (jnp.einsum('ifg,igr->ifr', self_score_gradient, self_block_keys) * scale_factor).reshape(CLEAN_TOKENS, HEAD_SIZE)
    self_key_contribution = (jnp.einsum('urs,urh->ush', self_score_gradient, self_block_queries) * scale_factor).reshape(CLEAN_TOKENS, HEAD_SIZE)
    query_grad = jnp.stack([clean_query, noisy_query + self_query_contribution])
    key_grad = jnp.stack([clean_key + noisy_key, self_key_contribution])
    value_grad = jnp.stack([clean_value + noisy_value, self_value_contribution])
    return (query_grad.astype(jnp.bfloat16), key_grad.astype(jnp.bfloat16), value_grad.astype(jnp.bfloat16))

def split_heads(array):
    return array.reshape(2, CLEAN_TOKENS, HEADS, HEAD_SIZE).transpose(2, 0, 1, 3)

def merge_heads(array):
    return array.transpose(1, 2, 0, 3).reshape(2, CLEAN_TOKENS, INNER)

def reference(queries, keys, values, block_order, out_weight, out_grad):
    causal, earlier = visibility(block_order)
    query_heads = split_heads(queries)
    key_heads = split_heads(keys)
    value_heads = split_heads(values)
    attention_heads, total_heads = lax.map(lambda head_items: head_forward(head_items[0], head_items[1], head_items[2], causal, earlier), (query_heads, key_heads, value_heads))
    attention = merge_heads(attention_heads)
    flat_attention = attention.reshape(2 * CLEAN_TOKENS, INNER)
    mixed_total = jnp.zeros((2 * CLEAN_TOKENS, D), jnp.float32)
    for group_index in range(N_TP):
        first_column = group_index * INNER_DEV
        group_sum = jnp.dot(flat_attention[:, first_column:first_column + INNER_DEV], out_weight[first_column:first_column + INNER_DEV], preferred_element_type=jnp.float32)
        mixed_total = mixed_total + rounded_result(group_sum)
    mixed = mixed_total.astype(jnp.bfloat16).reshape(2, CLEAN_TOKENS, D)
    flat_grad = out_grad.reshape(2 * CLEAN_TOKENS, D)
    head_grad = jnp.dot(flat_grad, out_weight.T, preferred_element_type=jnp.float32).astype(jnp.bfloat16)
    weight_grad = jnp.dot(flat_attention.T, flat_grad, preferred_element_type=jnp.float32)
    grad_heads = split_heads(head_grad.reshape(2, CLEAN_TOKENS, INNER))
    query_parts, key_parts, value_parts = lax.map(lambda head_items: head_backward(head_items[0], head_items[1], head_items[2], head_items[3], head_items[4], head_items[5], causal, earlier), (query_heads, key_heads, value_heads, attention_heads, grad_heads, total_heads))
    return (mixed, merge_heads(query_parts), merge_heads(key_parts), merge_heads(value_parts), weight_grad)
```

```python
import functools
import math

import jax
import jax.numpy as jnp
from jax import lax
from jax.experimental import pallas as pl
from jax.experimental.pallas import tpu as pltpu
from jax.sharding import PartitionSpec as P

HEAD_SIZE = 128
BLOCK = 16
HEADS_DEV = 3
ROWS = 256
BOTH = 2 * ROWS
POS_ROWS = ROWS // BLOCK
INNER_DEV = HEADS_DEV * HEAD_SIZE
WIDTH = 640
MESH = pl.DeviceIdType.MESH
F32 = jnp.float32
BF16 = jnp.bfloat16
MASKED = -1e30
LOWEST = -1e29
LOG2_SCALE = math.log2(math.e) / math.sqrt(HEAD_SIZE)
SCALE = 1.0 / math.sqrt(HEAD_SIZE)


def dot(a, b):
    return lax.dot_general(a, b, (((1,), (0,)), ((), ())), preferred_element_type=F32)


def dot_nt(a, b):
    return lax.dot_general(a, b, (((1,), (1,)), ((), ())), preferred_element_type=F32)


def dot_tn(a, b):
    return lax.dot_general(a, b, (((0,), (0,)), ((), ())), preferred_element_type=F32)


def remote(src, dst, send_sem, recv_sem, device):
    return pltpu.make_async_remote_copy(
        src_ref=src,
        dst_ref=dst,
        send_sem=send_sem,
        recv_sem=recv_sem,
        device_id=device,
        device_id_type=MESH,
    )


class RingReduce:
    def __init__(self, piece, via, ring, cross, send, recv, plus, minus, partner):
        self.piece, self.via, self.ring, self.cross = piece, via, ring, cross
        self.send, self.recv = send, recv
        self.plus, self.minus, self.partner = plus, minus, partner

    def copy(self, kind, p, n):
        if kind == "cross":
            return remote(
                self.piece(1, 0), self.cross, self.send.at[12], self.recv.at[12], self.partner
            )
        at = 6 * p + 2 * ("far", "near", "joint").index(kind) + n
        half = 1 - n if kind == "near" else n
        source = self.piece(p, 2 if kind == "far" else (1, 3)[n]).at[half]
        target = self.via.at[p, n] if kind == "far" else self.ring.at[p, n, half]
        device = (self.plus, self.minus)[n]
        return remote(source, target, self.send.at[at], self.recv.at[at], device)

    def start(self, kind, p, which=(0, 1)):
        for n in which:
            self.copy(kind, p, n).start()

    def join(self, p, which=(0, 1)):
        for n in which:
            self.copy("far", p, n).wait_recv()
            target = self.piece(p, (1, 3)[n])
            target[n] = (target[n].astype(F32) + self.via[p, n].astype(F32)).astype(BF16)
            self.copy("joint", p, n).start()

    def gathered(self, p):
        for kind in ("near", "joint"):
            for n in (0, 1):
                self.copy(kind, p, n).wait_recv()
        own = self.piece(p, 0)
        return own[...].astype(F32) + self.ring[p, 0].astype(F32) + self.ring[p, 1].astype(F32)

    def to_partner(self):
        total = self.gathered(1)
        self.piece(1, 0)[...] = total.astype(BF16)
        self.copy("cross", 1, 0).start()

    def result(self):
        total = self.gathered(0)
        self.copy("cross", 1, 0).wait_recv()
        return total + self.cross[...].astype(F32)

    def finish(self):
        for p in (0, 1):
            for kind in ("far", "near", "joint"):
                for n in (0, 1):
                    self.copy(kind, p, n).wait_send()
        self.copy("cross", 1, 0).wait_send()


def layer_kernel(
    q_ref, own_kv, noisy_kv, w_ref, og_ref, limit_ref,
    mixed_ref, qg_ref, kg_ref, vg_ref, wg_ref,
    kv, og, qt, acc, stat, att_t, att, bias, head_t, head, dq,
    mixp, m_via, m_ring, m_cross,
    w_pair, w_out, w_recv, w_via, w_ring, w_cross, w_final, w_other,
    t_out, t_recv, t_mine, t_via, t_ring, t_cross,
    kv_send, kv_recv, og_send, og_recv,
    m_send, m_rsem, w_send, w_rsem, ws_send, ws_recv, wf_sem,
    t_send, t_rsem, ts_send, ts_recv,
):
    s = lax.axis_index("seq")
    t = lax.axis_index("tp")
    y, x, c = s // 4, (s // 2) % 2, s % 2
    xh, z = t // 4, t % 4

    def slot(ys, xs, cs):
        return (ys * 2 + xs) * 2 + cs

    y_plus = {"seq": slot((y + 1) % 4, x, c)}
    y_minus = {"seq": slot((y + 3) % 4, x, c)}
    x_near = {"seq": slot(y, 1 - x, c)}
    sibling = {"seq": slot(y, x, 1 - c)}
    z_plus = {"tp": xh * 4 + (z + 1) % 4}
    z_minus = {"tp": xh * 4 + (z + 3) % 4}
    x_far = {"tp": (1 - xh) * 4 + z}

    barrier = pltpu.get_barrier_semaphore()
    partners = (y_plus, y_minus, x_near, sibling, z_plus, z_minus, x_far)
    for partner in partners:
        pl.semaphore_signal(barrier, inc=1, device_id=partner, device_id_type=MESH)
    kv[s] = own_kv[...]
    og[t] = og_ref[...]
    pl.semaphore_wait(barrier, len(partners))

    def kv_copy(place, half, sem, device):
        part = kv.at[place, half]
        return remote(part, part, kv_send.at[sem], kv_recv.at[place, half], device)

    def kv_pair(place, sem, device):
        return [kv_copy(place, half, sem + half, device) for half in (0, 1)]

    near_place = slot(y, 1 - x, c)
    x_copies = kv_pair(s, 16, x_near)
    own_plus, own_minus = kv_pair(s, 18, y_plus), kv_pair(s, 20, y_minus)
    near_plus, near_minus = kv_pair(near_place, 22, y_plus), kv_pair(near_place, 24, y_minus)

    def ring_place(p, off):
        return slot((y + off) % 4, (x + p) % 2, c)

    def pass_plus(p):
        return kv_copy(ring_place(p, 3), 0, 26 + 2 * p, y_plus)

    def pass_minus(p):
        return kv_copy(ring_place(p, 1), 1, 27 + 2 * p, y_minus)

    def og_copy(place, half, sem, device):
        part = og.at[place, half]
        return remote(part, part, og_send.at[sem], og_recv.at[place, half], device)

    def og_pair(place, sem, device):
        return [og_copy(place, half, sem + half, device) for half in (0, 1)]

    far_place = (1 - xh) * 4 + z
    og_far = og_pair(t, 0, x_far)
    og_own_plus, og_own_minus = og_pair(t, 2, z_plus), og_pair(t, 4, z_minus)
    og_far_plus, og_far_minus = og_pair(far_place, 6, z_plus), og_pair(far_place, 8, z_minus)

    def og_place(a, off):
        return ((xh + a) % 2) * 4 + (z + off) % 4

    def og_pass_plus(a):
        return og_copy(og_place(a, 3), 0, 10 + 2 * a, z_plus)

    def og_pass_minus(a):
        return og_copy(og_place(a, 1), 1, 11 + 2 * a, z_minus)

    def og_wait(place):
        for half in (0, 1):
            og_copy(place, half, 0, z_plus).wait_recv()

    for copy in (
        x_copies[0], x_copies[1], own_plus[0], own_minus[1], own_plus[1], own_minus[0],
        *kv_pair(s, 0, sibling),
        og_far[0], og_far[1], og_own_plus[0], og_own_minus[1], og_own_plus[1], og_own_minus[0],
    ):
        copy.start()

    for h in range(HEADS_DEV):
        cols = slice(h * HEAD_SIZE, (h + 1) * HEAD_SIZE)
        scaled = q_ref[:, cols].astype(F32).T * LOG2_SCALE
        high = scaled.astype(BF16)
        qt[h, :HEAD_SIZE] = high
        qt[h, HEAD_SIZE:] = (scaled - high.astype(F32)).astype(BF16)

    def cols_of(h):
        return slice(h * HEAD_SIZE, (h + 1) * HEAD_SIZE)

    def scores_of(key, h, first):
        return dot(jnp.concatenate([key, key], axis=1), qt[h, :, first:])

    row_block = lax.broadcasted_iota(jnp.int32, (ROWS, ROWS), 0) // BLOCK
    col_block = lax.broadcasted_iota(jnp.int32, (ROWS, ROWS), 1) // BLOCK
    self_bias = jnp.where(row_block == col_block, 0.0, MASKED).astype(F32)
    bias[:, :ROWS] = self_bias

    for h in range(HEADS_DEV):
        scores = scores_of(noisy_kv[0, :, cols_of(h)], h, ROWS) + bias[:, :ROWS]
        top = jnp.max(scores, axis=0, keepdims=True)
        weights = jnp.exp2(scores - top)
        stat[0, h : h + 1, :ROWS] = jnp.full((1, ROWS), LOWEST, F32)
        stat[0, h : h + 1, ROWS:] = top
        stat[1, h : h + 1, :ROWS] = jnp.zeros((1, ROWS), F32)
        stat[1, h : h + 1, ROWS:] = jnp.sum(weights, axis=0, keepdims=True)
        acc[cols_of(h), :ROWS] = jnp.zeros((HEAD_SIZE, ROWS), F32)
        acc[cols_of(h), ROWS:] = dot_tn(noisy_kv[1, :, cols_of(h)], weights.astype(BF16))

    def set_bias(place):
        position = kv[place, 0, ROWS:, :HEAD_SIZE].astype(F32)
        offset = lax.broadcasted_iota(jnp.int32, (BLOCK, HEAD_SIZE), 0).astype(F32)
        for b in range(POS_ROWS):
            code = position[b : b + 1] * float(BLOCK) + offset
            for n in range(BOTH // HEAD_SIZE):
                lanes = slice(n * HEAD_SIZE, (n + 1) * HEAD_SIZE)
                bias[b * BLOCK : (b + 1) * BLOCK, lanes] = jnp.where(
                    code <= limit_ref[0:1, lanes], 0.0, MASKED
                ).astype(F32)

    def forward_step(i, carry):
        g, d, e = i // 4, (i % 4) // 2, i % 2
        mid = ((g + 1) % 4) // 2
        p = (1 - mid) * e + mid * (g - 1)
        off = mid * (3 - 2 * e) + (1 - mid) * 2 * (g // 3)
        place = slot((y + off) % 4, (x + p) % 2, (c + d) % 2)

        @pl.when(i == 8)
        def _():
            og_wait(og_place(0, 3))
            og_pass_plus(0).start()
            og_wait(og_place(0, 1))
            og_pass_minus(0).start()

        @pl.when(i == 12)
        def _():
            og_wait(far_place)
            for n in (0, 1):
                og_far_plus[n].start()
                og_far_minus[1 - n].start()

        @pl.when(i > 0)
        def _():
            for half in (0, 1):
                kv_copy(place, half, 0, sibling).wait_recv()

        @pl.when(i == 1)
        def _():
            for n in (0, 1):
                near_plus[n].start()
                near_minus[1 - n].start()

        for p_now, at in ((0, 4), (1, 8)):

            @pl.when(i == at)
            def _():
                pass_plus(p_now).start()

            @pl.when(i == at + 1)
            def _():
                pass_minus(p_now).start()

        @pl.when((i > 0) & (d == 0))
        def _():
            for copy in kv_pair(place, 2 * (2 * g + e), sibling):
                copy.start()

        set_bias(place)
        for h in range(HEADS_DEV):
            scores = scores_of(kv[place, 0, :ROWS, cols_of(h)], h, 0) + bias[...]
            old = stat[0, h : h + 1]
            top = jnp.maximum(old, jnp.max(scores, axis=0, keepdims=True))
            weights = jnp.exp2(scores - top)
            factor = jnp.exp2(old - top)
            stat[0, h : h + 1] = top
            stat[1, h : h + 1] = stat[1, h : h + 1] * factor + jnp.sum(
                weights, axis=0, keepdims=True
            )
            acc[cols_of(h)] = acc[cols_of(h)] * factor + dot_tn(
                kv[place, 1, :ROWS, cols_of(h)], weights.astype(BF16)
            )
        return carry

    lax.fori_loop(0, 16, forward_step, 0)

    for h in range(HEADS_DEV):
        total = stat[1, h : h + 1]
        out = acc[cols_of(h)] / total
        att_t[cols_of(h)] = out.astype(BF16)
        att[:, cols_of(h)] = out.T.astype(BF16)
        stat[0, h : h + 1] = stat[0, h : h + 1] + jnp.log2(total)

    def columns(j):
        return pl.ds(pl.multiple_of(j * WIDTH, HEAD_SIZE), WIDTH)

    def mix_step(j, carry):
        mixp[j] = dot(att[...], w_ref[:, columns(j)]).astype(BF16).reshape(2, ROWS, WIDTH)
        return carry

    lax.fori_loop(0, 8, mix_step, 0)

    half_rows = INNER_DEV // 2
    head_t[...] = jnp.zeros((INNER_DEV, BOTH), F32)

    def w_copy(j):
        return remote(w_out.at[j], w_recv.at[j], ws_send.at[j], ws_recv.at[j], sibling)

    def projection_step(k, carry):
        u = k // 6
        off = (1 - u) * ((3 * (k % 3)) % 5) + u * 2
        a = (1 - u) * (k // 3) + u * (k - 6)
        j = og_place(a, off)

        @pl.when(k >= 4)
        def _():
            og_wait(j)

        @pl.when(k == 4)
        def _():
            og_pass_plus(1).start()

        @pl.when(k == 5)
        def _():
            og_pass_minus(1).start()

        grads = og[j].reshape(BOTH, WIDTH)
        head_t[...] += dot_nt(w_ref[:, columns(j)], grads)
        theirs = att_t[pl.ds(pl.multiple_of((1 - c) * half_rows, 16), half_rows)]
        w_out[j] = dot(theirs, grads).astype(BF16).reshape(2, half_rows // 2, WIDTH)
        w_copy(j).start()
        mine = att_t[pl.ds(pl.multiple_of(c * half_rows, 16), half_rows)]
        w_pair[j] = dot(mine, grads).astype(BF16).reshape(2, half_rows // 2, WIDTH)
        return carry

    lax.fori_loop(0, 8, projection_step, 0)

    mix = RingReduce(
        lambda p, r: mixp.at[og_place(p, r)], m_via, m_ring, m_cross, m_send, m_rsem,
        z_plus, z_minus, x_far,
    )
    weight = RingReduce(
        lambda p, r: w_pair.at[((y + r) % 4) * 2 + (x + p) % 2], w_via, w_ring, w_cross,
        w_send, w_rsem, y_plus, y_minus, x_near,
    )
    turns = [(1, 2), (0, 2), (1, 1), (1, 3), (0, 1), (0, 3), (1, 0), (0, 0)]
    term = RingReduce(
        lambda p, r: t_recv.at[turns.index((p, r))], t_via, t_ring, t_cross,
        t_send, t_rsem, y_plus, y_minus, x_near,
    )

    for p in (1, 0):
        mix.start("far", p)
        mix.start("near", p)

    for h in range(HEADS_DEV):
        grad = head_t[cols_of(h)]
        rounded = grad.astype(BF16)
        head[:, cols_of(h)] = grad.T.astype(BF16)
        stat[1, h : h + 1] = jnp.sum(
            rounded.astype(F32) * att_t[cols_of(h)].astype(F32), axis=0, keepdims=True
        )
        att_t[cols_of(h)] = rounded
        dq[cols_of(h)] = jnp.zeros((HEAD_SIZE, BOTH), F32)
    head_tb = att_t

    def w_sum(j, carry):
        w_copy(j).wait_recv()
        w_pair[j] = (w_pair[j].astype(F32) + w_recv[j].astype(F32)).astype(BF16)
        return carry

    lax.fori_loop(0, 8, w_sum, 0)
    for p in (1, 0):
        weight.start("far", p)
        weight.start("near", p)

    def backward_tile(key, value, h, first, masks):
        scores = scores_of(key, h, first) + masks
        probs = jnp.exp2(scores - stat[0, h : h + 1, first:])
        value_term = dot(probs.astype(BF16), head[first:, cols_of(h)])
        prob_grad = dot(value, head_tb[cols_of(h), first:])
        score_grad = (probs * (prob_grad - stat[1, h : h + 1, first:])).astype(BF16)
        key_term = dot(score_grad, q_ref[first:, cols_of(h)]) * SCALE
        dq[cols_of(h), first:] += dot_tn(key, score_grad)
        return key_term.astype(BF16), value_term.astype(BF16)

    bias[:, :ROWS] = self_bias
    for h in range(HEADS_DEV):
        key_term, value_term = backward_tile(
            noisy_kv[0, :, cols_of(h)], noisy_kv[1, :, cols_of(h)], h, ROWS, bias[:, :ROWS]
        )
        kg_ref[1, :, cols_of(h)] = key_term
        vg_ref[1, :, cols_of(h)] = value_term

    def t_copy(j):
        return remote(t_out.at[j], t_recv.at[j], ts_send.at[j], ts_recv.at[j], sibling)

    def backward_step(i, carry):
        j, d = i // 2, 1 - i % 2
        g, e = j // 2, j % 2
        mid = ((g + 1) % 4) // 2
        off = mid * (1 + 2 * e) + (1 - mid) * 2 * (1 - g // 3)
        p = mid * (2 - g) + (1 - mid) * (1 - e)
        place = slot((y + off) % 4, (x + p) % 2, (c + d) % 2)

        @pl.when(i == 2)
        def _():
            weight.join(1)
            weight.join(0)

        @pl.when(i == 5)
        def _():
            mix.join(1)

        @pl.when(i == 9)
        def _():
            weight.to_partner()

        @pl.when(i == 10)
        def _():
            mix.join(0)

        @pl.when(i == 14)
        def _():
            term.to_partner()

        set_bias(place)
        for h in range(HEADS_DEV):
            key_term, value_term = backward_tile(
                kv[place, 0, :ROWS, cols_of(h)], kv[place, 1, :ROWS, cols_of(h)], h, 0, bias[...]
            )
            t_mine[0, :, cols_of(h)] = key_term
            t_mine[1, :, cols_of(h)] = value_term

        @pl.when(d == 1)
        def _():
            t_out[j] = t_mine[...]
            t_copy(j).start()

        @pl.when(d == 0)
        def _():
            t_copy(j).wait_recv()
            t_recv[j] = (t_recv[j].astype(F32) + t_mine[...].astype(F32)).astype(BF16)

        for n, (p_now, r) in enumerate(turns):
            if r == 0:
                continue

            @pl.when(i == 2 * n + 1)
            def _():
                if r == 2:
                    term.start("far", p_now)
                else:
                    which = (0,) if r == 1 else (1,)
                    term.start("near", p_now, which)
                    term.join(p_now, which)

        return carry

    lax.fori_loop(0, 16, backward_step, 0)

    for h in range(HEADS_DEV):
        qg_ref[:, cols_of(h)] = (dq[cols_of(h)] * SCALE).T.astype(BF16)

    mix.to_partner()

    w_final[...] = weight.result().reshape(half_rows, WIDTH)
    final_copy = remote(w_final, w_other, wf_sem.at[0], wf_sem.at[1], sibling)
    final_copy.start()

    terms = term.result().astype(BF16)
    kg_ref[0] = terms[0]
    vg_ref[0] = terms[1]

    final_copy.wait_recv()
    wg_ref[pl.ds(pl.multiple_of(c * half_rows, 16), half_rows)] = w_final[...]
    wg_ref[pl.ds(pl.multiple_of((1 - c) * half_rows, 16), half_rows)] = w_other[...]

    mixed_ref[...] = mix.result().astype(BF16)

    for copy in (*x_copies, *own_plus, *own_minus, *near_plus, *near_minus):
        copy.wait_send()
    for n in range(8):
        for copy in kv_pair(s, 2 * n, sibling):
            copy.wait_send()
        w_copy(n).wait_send()
        t_copy(n).wait_send()
    for p in (0, 1):
        pass_plus(p).wait_send()
        pass_minus(p).wait_send()
        og_pass_plus(p).wait_send()
        og_pass_minus(p).wait_send()
    for copy in (*og_far, *og_own_plus, *og_own_minus, *og_far_plus, *og_far_minus):
        copy.wait_send()
    mix.finish()
    weight.finish()
    term.finish()
    final_copy.wait_send()


def local(queries, keys, values, block_order, out_weight, out_grad):
    position = block_order.astype(F32)
    marks = jnp.broadcast_to(position.astype(BF16)[:, None], (POS_ROWS, INNER_DEV))
    own_kv = jnp.stack([jnp.concatenate([a[0], marks], axis=0) for a in (keys, values)])
    noisy_kv = jnp.stack([keys[1], values[1]])
    first = jnp.repeat(position * BLOCK, BLOCK)
    offsets = jnp.tile(jnp.arange(BLOCK, dtype=F32), POS_ROWS)
    limit = jnp.broadcast_to(jnp.concatenate([first + offsets, first - 1.0]), (8, BOTH))
    unit = (2, ROWS, INNER_DEV)
    w_unit = (2, INNER_DEV // 4, WIDTH)
    m_unit = (2, ROWS, WIDTH)

    def buffer(*shape, dtype=BF16):
        return pltpu.VMEM(shape, dtype)

    def sums(u):
        return [buffer(2, *u), buffer(2, 2, *u), buffer(*u)]

    scratch = [
        buffer(16, 2, ROWS + POS_ROWS, INNER_DEV),
        buffer(8, *m_unit),
        buffer(HEADS_DEV, 2 * HEAD_SIZE, BOTH),
        buffer(INNER_DEV, BOTH, dtype=F32),
        buffer(2, 8, BOTH, dtype=F32),
        buffer(INNER_DEV, BOTH),
        buffer(BOTH, INNER_DEV),
        buffer(ROWS, BOTH, dtype=F32),
        buffer(INNER_DEV, BOTH, dtype=F32),
        buffer(BOTH, INNER_DEV),
        buffer(INNER_DEV, BOTH, dtype=F32),
        buffer(8, *m_unit), *sums(m_unit),
        buffer(8, *w_unit), buffer(8, *w_unit), buffer(8, *w_unit), *sums(w_unit),
        buffer(INNER_DEV // 2, WIDTH, dtype=F32), buffer(INNER_DEV // 2, WIDTH, dtype=F32),
        buffer(8, *unit), buffer(8, *unit), buffer(*unit), *sums(unit),
        pltpu.SemaphoreType.DMA((30,)), pltpu.SemaphoreType.DMA((16, 2)),
        pltpu.SemaphoreType.DMA((14,)), pltpu.SemaphoreType.DMA((8, 2)),
        pltpu.SemaphoreType.DMA((13,)), pltpu.SemaphoreType.DMA((13,)),
        pltpu.SemaphoreType.DMA((13,)), pltpu.SemaphoreType.DMA((13,)),
        pltpu.SemaphoreType.DMA((8,)), pltpu.SemaphoreType.DMA((8,)),
        pltpu.SemaphoreType.DMA((2,)),
        pltpu.SemaphoreType.DMA((13,)), pltpu.SemaphoreType.DMA((13,)),
        pltpu.SemaphoreType.DMA((8,)), pltpu.SemaphoreType.DMA((8,)),
    ]
    whole = pl.BlockSpec(memory_space=pltpu.VMEM)
    mixed, query_grad, key_grad, value_grad, weight_grad = pl.pallas_call(
        layer_kernel,
        out_shape=(
            jax.ShapeDtypeStruct(m_unit, BF16),
            jax.ShapeDtypeStruct((BOTH, INNER_DEV), BF16),
            jax.ShapeDtypeStruct(unit, BF16),
            jax.ShapeDtypeStruct(unit, BF16),
            jax.ShapeDtypeStruct((INNER_DEV, WIDTH), F32),
        ),
        in_specs=[whole] * 6,
        out_specs=(whole,) * 5,
        scratch_shapes=scratch,
        compiler_params=pltpu.CompilerParams(
            collective_id=0, has_side_effects=True, vmem_limit_bytes=63 * 2**20
        ),
    )(queries.reshape(BOTH, INNER_DEV), own_kv, noisy_kv, out_weight, out_grad, limit)
    core = lax.axis_index("seq") % 2
    weight_grad = lax.dynamic_slice_in_dim(weight_grad, core * (WIDTH // 2), WIDTH // 2, axis=1)
    return (mixed, query_grad.reshape(unit), key_grad, value_grad, weight_grad)


def solution(mesh):
    return jax.shard_map(
        local,
        mesh=mesh,
        in_specs=(
            P(None, "seq", "tp"),
            P(None, "seq", "tp"),
            P(None, "seq", "tp"),
            P("seq"),
            P("tp", None),
            P(None, "seq", "tp"),
        ),
        out_specs=(
            P(None, "seq", "tp"),
            P(None, "seq", "tp"),
            P(None, "seq", "tp"),
            P(None, "seq", "tp"),
            P("tp", "seq"),
        ),
        check_vma=False,
    )
```

```python
import functools
import math

import jax
import jax.numpy as jnp
from jax import lax
from jax.experimental import pallas as pl
from jax.experimental.pallas import tpu as pltpu
from jax.sharding import PartitionSpec as P

HEAD_SIZE = 128
BLOCK = 16
HEADS_DEV = 3
ROWS = 256
BOTH = 2 * ROWS
POS_ROWS = ROWS // BLOCK
INNER_DEV = HEADS_DEV * HEAD_SIZE
WIDTH = 640
MESH = pl.DeviceIdType.MESH
F32 = jnp.float32
BF16 = jnp.bfloat16
MASKED = -1e30
LOWEST = -1e29
LOG2_SCALE = math.log2(math.e) / math.sqrt(HEAD_SIZE)
SCALE = 1.0 / math.sqrt(HEAD_SIZE)


def dot(a, b):
    return lax.dot_general(a, b, (((1,), (0,)), ((), ())), preferred_element_type=F32)


def dot_nt(a, b):
    return lax.dot_general(a, b, (((1,), (1,)), ((), ())), preferred_element_type=F32)


def dot_tn(a, b):
    return lax.dot_general(a, b, (((0,), (0,)), ((), ())), preferred_element_type=F32)


def remote(src, dst, send_sem, recv_sem, device):
    return pltpu.make_async_remote_copy(
        src_ref=src,
        dst_ref=dst,
        send_sem=send_sem,
        recv_sem=recv_sem,
        device_id=device,
        device_id_type=MESH,
    )


def equal(a, n):
    return (a + 16 - n) // 16 - (a + 15 - n) // 16


class RingReduce:
    def __init__(self, piece, via, ring, cross, send, recv, plus, minus, partner):
        self.piece, self.via, self.ring, self.cross = piece, via, ring, cross
        self.send, self.recv = send, recv
        self.plus, self.minus, self.partner = plus, minus, partner

    def copy(self, kind, p, n):
        if kind == "cross":
            return remote(
                self.piece(1, 0), self.cross, self.send.at[12], self.recv.at[12], self.partner
            )
        at = 6 * p + 2 * ("far", "near", "joint").index(kind) + n
        half = 1 - n if kind == "near" else n
        source = self.piece(p, 2 if kind == "far" else (1, 3)[n]).at[half]
        target = self.via.at[p, n] if kind == "far" else self.ring.at[p, n, half]
        device = (self.plus, self.minus)[n]
        return remote(source, target, self.send.at[at], self.recv.at[at], device)

    def start(self, kind, p, which=(0, 1)):
        for n in which:
            self.copy(kind, p, n).start()

    def join(self, p, which=(0, 1)):
        for n in which:
            self.copy("far", p, n).wait_recv()
            target = self.piece(p, (1, 3)[n])
            target[n] = (target[n].astype(F32) + self.via[p, n].astype(F32)).astype(BF16)
            self.copy("joint", p, n).start()

    def gathered(self, p):
        for kind in ("near", "joint"):
            for n in (0, 1):
                self.copy(kind, p, n).wait_recv()
        own = self.piece(p, 0)
        return own[...].astype(F32) + self.ring[p, 0].astype(F32) + self.ring[p, 1].astype(F32)

    def to_partner(self):
        total = self.gathered(1)
        self.piece(1, 0)[...] = total.astype(BF16)
        self.copy("cross", 1, 0).start()

    def result(self):
        total = self.gathered(0)
        self.copy("cross", 1, 0).wait_recv()
        return total + self.cross[...].astype(F32)

    def finish(self, sides=(0, 1)):
        for p in sides:
            for kind in ("far", "near", "joint"):
                for n in (0, 1):
                    self.copy(kind, p, n).wait_send()
        if 1 in sides:
            self.copy("cross", 1, 0).wait_send()


def layer_kernel(
    order_ref, q_ref, k_ref, v_ref, weight_ref, og_ref,
    mixed_ref, qg_ref, kg_ref, vg_ref, wg_ref,
    kv, noisy_kv, w_ref, og, limit, qt, acc, stat, att_t, att, bias, head_t, head, dq,
    mixp, m_via, m_ring, m_cross,
    w_pair, w_out, w_recv, w_x, w_via, w_ring, w_final, w_turn,
    t_out, t_recv, t_mine, t_via, t_ring, t_cross,
    load, kv_send, kv_recv, og_send, og_recv,
    m_send, m_rsem, w_send, w_rsem, ws_send, ws_recv, wx_send, wx_recv, wf_sem,
    t_send, t_rsem, ts_send, ts_recv,
):
    s = lax.axis_index("seq")
    t = lax.axis_index("tp")
    y, x, c = s // 4, (s // 2) % 2, s % 2
    xh, z = t // 4, t % 4

    def slot(ys, xs, cs):
        return (ys * 2 + xs) * 2 + cs

    y_plus = {"seq": slot((y + 1) % 4, x, c)}
    y_minus = {"seq": slot((y + 3) % 4, x, c)}
    x_near = {"seq": slot(y, 1 - x, c)}
    sibling = {"seq": slot(y, x, 1 - c)}
    z_plus = {"tp": xh * 4 + (z + 1) % 4}
    z_minus = {"tp": xh * 4 + (z + 3) % 4}
    x_far = {"tp": (1 - xh) * 4 + z}

    barrier = pltpu.get_barrier_semaphore()
    partners = (y_plus, y_minus, x_near, sibling, z_plus, z_minus, x_far)
    for partner in partners:
        pl.semaphore_signal(barrier, inc=1, device_id=partner, device_id_type=MESH)

    loads = [
        pltpu.make_async_copy(src, dst, load.at[n])
        for n, (src, dst) in enumerate(
            (
                (k_ref.at[0], kv.at[s, 0, pl.ds(0, ROWS)]),
                (v_ref.at[0], kv.at[s, 1, pl.ds(0, ROWS)]),
                (og_ref, og.at[t]),
                (k_ref.at[1], noisy_kv.at[0]),
                (v_ref.at[1], noisy_kv.at[1]),
                (weight_ref, w_ref),
            )
        )
    ]
    for copy in loads:
        copy.start()

    mark_row = lax.broadcasted_iota(jnp.int32, (POS_ROWS, INNER_DEV), 0)
    lane = lax.broadcasted_iota(jnp.int32, (8, BOTH), 1)
    lane_block = (lane % ROWS) // BLOCK
    marks = jnp.zeros((POS_ROWS, INNER_DEV), F32)
    start = jnp.zeros((8, BOTH), F32)
    for b in range(POS_ROWS):
        position = order_ref[b].astype(F32)
        marks = jnp.where(mark_row == b, position, marks)
        start = jnp.where(lane_block == b, position * float(BLOCK), start)
    kv[s, 0, ROWS:] = marks.astype(BF16)
    kv[s, 1, ROWS:] = marks.astype(BF16)
    limit[...] = start + jnp.where(lane < ROWS, lane % BLOCK, -1).astype(F32)

    def kv_copy(place, half, sem, device):
        part = kv.at[place, half]
        return remote(part, part, kv_send.at[sem], kv_recv.at[place, half], device)

    near_place = slot(y, 1 - x, c)

    def ring_place(p, off):
        return slot((y + off) % 4, (x + p) % 2, c)

    def own_copy(kind, half):
        at = {"sibling": 0, "x": 16, "plus": 18, "minus": 20}[kind] + half
        device = {"sibling": sibling, "x": x_near, "plus": y_plus, "minus": y_minus}[kind]
        return kv_copy(s, half, at, device)

    def near_copy(kind, half):
        at = {"plus": 22, "minus": 24}[kind] + half
        return kv_copy(near_place, half, at, {"plus": y_plus, "minus": y_minus}[kind])

    def pass_plus(p):
        return kv_copy(ring_place(p, 3), 0, 26 + 2 * p, y_plus)

    def pass_minus(p):
        return kv_copy(ring_place(p, 1), 1, 27 + 2 * p, y_minus)

    def og_copy(place, half, sem, device):
        part = og.at[place, half]
        return remote(part, part, og_send.at[sem], og_recv.at[place, half], device)

    far_place = (1 - xh) * 4 + z

    def og_own(kind, half):
        at = {"far": 0, "plus": 2, "minus": 4}[kind] + half
        return og_copy(t, half, at, {"far": x_far, "plus": z_plus, "minus": z_minus}[kind])

    def og_far(kind, half):
        at = {"plus": 6, "minus": 8}[kind] + half
        return og_copy(far_place, half, at, {"plus": z_plus, "minus": z_minus}[kind])

    def og_place(a, off):
        return ((xh + a) % 2) * 4 + (z + off) % 4

    def og_pass_plus(a):
        return og_copy(og_place(a, 3), 0, 10 + 2 * a, z_plus)

    def og_pass_minus(a):
        return og_copy(og_place(a, 1), 1, 11 + 2 * a, z_minus)

    def og_wait(place, halves=(0, 1)):
        for half in halves:
            og_copy(place, half, 0, z_plus).wait_recv()

    loads[0].wait()
    loads[1].wait()
    loads[2].wait()
    pl.semaphore_wait(barrier, len(partners))
    for n in (0, 1):
        own_copy("x", n).start()
        own_copy("plus", n).start()
        own_copy("minus", 1 - n).start()
    for n in (0, 1):
        og_own("plus", n).start()
        og_own("minus", 1 - n).start()
        og_own("far", n).start()
        own_copy("sibling", n).start()

    for h in range(HEADS_DEV):
        cols = slice(h * HEAD_SIZE, (h + 1) * HEAD_SIZE)
        scaled = q_ref[:, cols].astype(F32).T * LOG2_SCALE
        high = scaled.astype(BF16)
        qt[h, :HEAD_SIZE] = high
        qt[h, HEAD_SIZE:] = (scaled - high.astype(F32)).astype(BF16)

    def cols_of(h):
        return slice(h * HEAD_SIZE, (h + 1) * HEAD_SIZE)

    def scores_of(key, h, first):
        return dot(jnp.concatenate([key, key], axis=1), qt[h, :, first:])

    loads[3].wait()
    loads[4].wait()
    row_block = lax.broadcasted_iota(jnp.int32, (ROWS, ROWS), 0) // BLOCK
    col_block = lax.broadcasted_iota(jnp.int32, (ROWS, ROWS), 1) // BLOCK
    self_bias = jnp.where(row_block == col_block, 0.0, MASKED).astype(F32)
    bias[:, :ROWS] = self_bias

    for h in range(HEADS_DEV):
        scores = scores_of(noisy_kv[0, :, cols_of(h)], h, ROWS) + bias[:, :ROWS]
        top = jnp.max(scores, axis=0, keepdims=True)
        weights = jnp.exp2(scores - top)
        stat[0, h : h + 1, :ROWS] = jnp.full((1, ROWS), LOWEST, F32)
        stat[0, h : h + 1, ROWS:] = top
        stat[1, h : h + 1, :ROWS] = jnp.zeros((1, ROWS), F32)
        stat[1, h : h + 1, ROWS:] = jnp.sum(weights, axis=0, keepdims=True)
        acc[cols_of(h), :ROWS] = jnp.zeros((HEAD_SIZE, ROWS), F32)
        acc[cols_of(h), ROWS:] = dot_tn(noisy_kv[1, :, cols_of(h)], weights.astype(BF16))

    def set_bias(place):
        position = kv[place, 0, ROWS:, :HEAD_SIZE].astype(F32)
        offset = lax.broadcasted_iota(jnp.int32, (BLOCK, HEAD_SIZE), 0).astype(F32)
        for b in range(POS_ROWS):
            code = position[b : b + 1] * float(BLOCK) + offset
            for n in range(BOTH // HEAD_SIZE):
                lanes = slice(n * HEAD_SIZE, (n + 1) * HEAD_SIZE)
                bias[b * BLOCK : (b + 1) * BLOCK, lanes] = jnp.where(
                    code <= limit[0:1, lanes], 0.0, MASKED
                ).astype(F32)

    def forward_step(i, carry):
        n, d = i // 2, i % 2
        p = n // 5 + (n + 6) // 7 - (n + 5) // 7
        m = (n + 1) % 3
        off = ((n + 6) // 8) * (m + 3 * ((2 - m) // 2))
        place = slot((y + off) % 4, (x + p) % 2, (c + d) % 2)

        @pl.when(i == 6)
        def _():
            og_wait(og_place(0, 3), (0,))
            og_pass_plus(0).start()
            og_wait(og_place(0, 1), (1,))
            og_pass_minus(0).start()

        @pl.when(i == 8)
        def _():
            og_wait(far_place, (0,))
            og_far("plus", 0).start()

        @pl.when(i == 10)
        def _():
            og_wait(far_place, (1,))
            og_far("minus", 1).start()
            og_far("plus", 1).start()
            og_far("minus", 0).start()

        for half in (0, 1):

            @pl.when(i > 0)
            def _():
                kv_copy(place, half, 0, sibling).wait_recv()

            @pl.when(i == 2)
            def _():
                near_copy("plus", half).start()
                near_copy("minus", half).start()

            for side, at in ((0, 4), (1, 10)):

                @pl.when(i == at + 2 * half)
                def _():
                    (pass_minus if half else pass_plus)(side).start()

            @pl.when((i > 0) & (d == 0))
            def _():
                kv_copy(place, half, 2 * n + half, sibling).start()

        set_bias(place)
        for h in range(HEADS_DEV):
            scores = scores_of(kv[place, 0, :ROWS, cols_of(h)], h, 0) + bias[...]
            old = stat[0, h : h + 1]
            top = jnp.maximum(old, jnp.max(scores, axis=0, keepdims=True))
            weights = jnp.exp2(scores - top)
            factor = jnp.exp2(old - top)
            stat[0, h : h + 1] = top
            stat[1, h : h + 1] = stat[1, h : h + 1] * factor + jnp.sum(
                weights, axis=0, keepdims=True
            )
            acc[cols_of(h)] = acc[cols_of(h)] * factor + dot_tn(
                kv[place, 1, :ROWS, cols_of(h)], weights.astype(BF16)
            )
        return carry

    lax.fori_loop(0, 16, forward_step, 0)
    og_wait(og_place(1, 3), (0,))
    og_pass_plus(1).start()
    og_wait(og_place(1, 1), (1,))
    og_pass_minus(1).start()

    for h in range(HEADS_DEV):
        total = stat[1, h : h + 1]
        out = acc[cols_of(h)] / total
        att_t[cols_of(h)] = out.astype(BF16)
        att[:, cols_of(h)] = out.T.astype(BF16)
        stat[0, h : h + 1] = stat[0, h : h + 1] + jnp.log2(total)

    def columns(j):
        return pl.ds(pl.multiple_of(j * WIDTH, HEAD_SIZE), WIDTH)

    loads[5].wait()

    def mix_step(j, carry):
        mixp[j] = dot(att[...], w_ref[:, columns(j)]).astype(BF16).reshape(2, ROWS, WIDTH)
        return carry

    lax.fori_loop(0, 8, mix_step, 0)

    half_rows = INNER_DEV // 2
    head_t[...] = jnp.zeros((INNER_DEV, BOTH), F32)

    def w_copy(j):
        return remote(w_out.at[j], w_recv.at[j], ws_send.at[j], ws_recv.at[j], sibling)

    def w_across(n):
        return remote(w_pair.at[2 * n + 1 - x], w_x.at[n], wx_send.at[n], wx_recv.at[n], x_near)

    def w_sum(j):
        w_copy(j).wait_recv()
        w_pair[j] = (w_pair[j].astype(F32) + w_recv[j].astype(F32)).astype(BF16)

        @pl.when(j % 2 == 1 - x)
        def _():
            w_across(j // 2).start()

    og_order = ((0, 0), (0, 3), (0, 1), (1, 0), (0, 2), (1, 3), (1, 1), (1, 2))

    def og_at(k):
        a = sum(u[0] * equal(k, n) for n, u in enumerate(og_order))
        off = sum(u[1] * equal(k, n) for n, u in enumerate(og_order))
        return og_place(a, off)

    def projection_step(k, carry):
        j = og_at(k)

        for half, pieces in enumerate(((2, 4, 6, 7), (1, 4, 5, 7))):
            for n in pieces:

                @pl.when(k == n)
                def _():
                    og_wait(j, (half,))

        grads = og[j].reshape(BOTH, WIDTH)
        theirs = att_t[pl.ds(pl.multiple_of((1 - c) * half_rows, 16), half_rows)]
        w_out[j] = dot(theirs, grads).astype(BF16).reshape(2, half_rows // 2, WIDTH)
        w_copy(j).start()
        mine = att_t[pl.ds(pl.multiple_of(c * half_rows, 16), half_rows)]
        w_pair[j] = dot(mine, grads).astype(BF16).reshape(2, half_rows // 2, WIDTH)
        head_t[...] += dot_nt(w_ref[:, columns(j)], grads)

        @pl.when(k > 0)
        def _():
            w_sum(og_at(k - 1))

        return carry

    mix = RingReduce(
        lambda p, r: mixp.at[og_place(p, r)], m_via, m_ring, m_cross, m_send, m_rsem,
        z_plus, z_minus, x_far,
    )
    weight = RingReduce(
        lambda p, r: w_pair.at[((y + r) % 4) * 2 + (x + p) % 2], w_via, w_ring, None,
        w_send, w_rsem, y_plus, y_minus, x_near,
    )
    mix.start("far", 1)
    mix.start("near", 1)
    lax.fori_loop(0, 8, projection_step, 0)
    w_sum(og_at(7))

    turns = [(1, 2), (1, 1), (1, 3), (1, 0), (0, 2), (0, 1), (0, 3), (0, 0)]
    term = RingReduce(
        lambda p, r: t_recv.at[turns.index((p, r))], t_via, t_ring, t_cross,
        t_send, t_rsem, y_plus, y_minus, x_near,
    )

    for h in range(HEADS_DEV):
        grad = head_t[cols_of(h)]
        rounded = grad.astype(BF16)
        head[:, cols_of(h)] = grad.T.astype(BF16)
        stat[1, h : h + 1] = jnp.sum(
            rounded.astype(F32) * att_t[cols_of(h)].astype(F32), axis=0, keepdims=True
        )
        att_t[cols_of(h)] = rounded
        dq[cols_of(h)] = jnp.zeros((HEAD_SIZE, BOTH), F32)
    head_tb = att_t

    def backward_tile(key, value, h, first, masks):
        scores = scores_of(key, h, first) + masks
        probs = jnp.exp2(scores - stat[0, h : h + 1, first:])
        value_term = dot(probs.astype(BF16), head[first:, cols_of(h)])
        prob_grad = dot(value, head_tb[cols_of(h), first:])
        score_grad = (probs * (prob_grad - stat[1, h : h + 1, first:])).astype(BF16)
        key_term = dot(score_grad, q_ref[first:, cols_of(h)]) * SCALE
        dq[cols_of(h), first:] += dot_tn(key, score_grad)
        return key_term.astype(BF16), value_term.astype(BF16)

    bias[:, :ROWS] = self_bias
    for h in range(HEADS_DEV):
        key_term, value_term = backward_tile(
            noisy_kv[0, :, cols_of(h)], noisy_kv[1, :, cols_of(h)], h, ROWS, bias[:, :ROWS]
        )
        kg_ref[1, :, cols_of(h)] = key_term
        vg_ref[1, :, cols_of(h)] = value_term

    def t_copy(j):
        return remote(t_out.at[j], t_recv.at[j], ts_send.at[j], ts_recv.at[j], sibling)

    w_mine = pl.multiple_of(c * half_rows, 16)

    def final_copy():
        part = w_final.at[pl.ds(w_mine, half_rows)]
        return remote(part, part, wf_sem.at[0], wf_sem.at[1], sibling)

    def backward_step(i, carry):
        j, d = i // 2, 1 - i % 2
        p, q = 1 - j // 4, j % 4
        off = 2 * equal(q, 0) + equal(q, 1) + 3 * equal(q, 2)
        place = slot((y + off) % 4, (x + p) % 2, (c + d) % 2)

        @pl.when(i == 2)
        def _():
            mix.join(1)
            mix.start("far", 0)
            mix.start("near", 0)

        @pl.when(i == 6)
        def _():
            for n in range(4):
                w_across(n).wait_recv()
                mine = w_pair.at[2 * n + x]
                mine[...] = (mine[...].astype(F32) + w_x[n].astype(F32)).astype(BF16)
            weight.start("far", 0)
            weight.start("near", 0)

        @pl.when(i == 10)
        def _():
            weight.join(0)

        @pl.when(i == 11)
        def _():
            term.to_partner()

        @pl.when(i == 12)
        def _():
            mix.to_partner()

        @pl.when(i == 14)
        def _():
            w_final[pl.ds(w_mine, half_rows)] = weight.gathered(0).reshape(half_rows, WIDTH)
            final_copy().start()

        set_bias(place)
        for h in range(HEADS_DEV):
            key_term, value_term = backward_tile(
                kv[place, 0, :ROWS, cols_of(h)], kv[place, 1, :ROWS, cols_of(h)], h, 0, bias[...]
            )
            t_mine[0, :, cols_of(h)] = key_term
            t_mine[1, :, cols_of(h)] = value_term

        @pl.when(d == 1)
        def _():
            t_out[j] = t_mine[...]
            t_copy(j).start()

        @pl.when(d == 0)
        def _():
            t_copy(j).wait_recv()
            t_recv[j] = (t_recv[j].astype(F32) + t_mine[...].astype(F32)).astype(BF16)

        for n, (p_now, r) in enumerate(turns):
            if r == 0:
                continue

            @pl.when(i == 2 * n + 1)
            def _():
                if r == 2:
                    term.start("far", p_now)
                else:
                    which = (0,) if r == 1 else (1,)
                    term.start("near", p_now, which)
                    term.join(p_now, which)

        return carry

    lax.fori_loop(0, 16, backward_step, 0)

    mix.join(0)
    for h in range(HEADS_DEV):
        qg_ref[:, cols_of(h)] = (dq[cols_of(h)] * SCALE).T.astype(BF16)


    w_theirs = pl.multiple_of((1 - c) * half_rows, 16)
    part = w_final.at[pl.ds(w_theirs, half_rows)]
    remote(part, part, wf_sem.at[0], wf_sem.at[1], sibling).wait_recv()
    for n in range(INNER_DEV // HEAD_SIZE):
        w_turn[:, cols_of(n)] = w_final[cols_of(n)].T
    wg_ref[...] = w_turn[pl.ds(pl.multiple_of(c * (WIDTH // 2), 8), WIDTH // 2)]

    terms = term.result().astype(BF16)
    kg_ref[0] = terms[0]
    vg_ref[0] = terms[1]

    mixed_ref[...] = mix.result().astype(BF16)

    for half in (0, 1):
        for kind in ("x", "plus", "minus"):
            own_copy(kind, half).wait_send()
        for kind in ("plus", "minus"):
            near_copy(kind, half).wait_send()
            og_own(kind, half).wait_send()
            og_far(kind, half).wait_send()
        og_own("far", half).wait_send()
        for n in range(8):
            kv_copy(s, half, 2 * n + half, sibling).wait_send()
    for n in range(8):
        w_copy(n).wait_send()
        t_copy(n).wait_send()
    for n in range(4):
        w_across(n).wait_send()
    for p in (0, 1):
        pass_plus(p).wait_send()
        pass_minus(p).wait_send()
        og_pass_plus(p).wait_send()
        og_pass_minus(p).wait_send()
    mix.finish()
    weight.finish((0,))
    term.finish()
    final_copy().wait_send()


def results_kernel(*refs):
    count = len(refs) // 2
    copies = [
        pltpu.make_async_copy(refs[n], refs[count + n], refs[-1].at[n]) for n in range(count)
    ]
    for copy in copies:
        copy.start()
    for copy in copies:
        copy.wait()


def local(queries, keys, values, block_order, out_weight, out_grad):
    unit = (2, ROWS, INNER_DEV)
    w_unit = (2, INNER_DEV // 4, WIDTH)
    m_unit = (2, ROWS, WIDTH)

    def buffer(*shape, dtype=BF16):
        return pltpu.VMEM(shape, dtype)

    def sums(u):
        return [buffer(2, *u), buffer(2, 2, *u), buffer(*u)]

    scratch = [
        buffer(16, 2, ROWS + POS_ROWS, INNER_DEV),
        buffer(*unit),
        buffer(*out_weight.shape),
        buffer(8, *m_unit),
        buffer(8, BOTH, dtype=F32),
        buffer(HEADS_DEV, 2 * HEAD_SIZE, BOTH),
        buffer(INNER_DEV, BOTH, dtype=F32),
        buffer(2, 8, BOTH, dtype=F32),
        buffer(INNER_DEV, BOTH),
        buffer(BOTH, INNER_DEV),
        buffer(ROWS, BOTH, dtype=F32),
        buffer(INNER_DEV, BOTH, dtype=F32),
        buffer(BOTH, INNER_DEV),
        buffer(INNER_DEV, BOTH, dtype=F32),
        buffer(8, *m_unit), *sums(m_unit),
        buffer(8, *w_unit), buffer(8, *w_unit), buffer(8, *w_unit), buffer(4, *w_unit),
        *sums(w_unit)[:2], buffer(INNER_DEV, WIDTH, dtype=F32),
        buffer(WIDTH, INNER_DEV, dtype=F32),
        buffer(8, *unit), buffer(8, *unit), buffer(*unit), *sums(unit),
        *(
            pltpu.SemaphoreType.DMA(shape)
            for shape in (
                (6,), (30,), (16, 2), (14,), (8, 2), (13,), (13,), (13,), (13,),
                (8,), (8,), (4,), (4,), (2,), (13,), (13,), (8,), (8,),
            )
        ),
    ]
    whole = pl.BlockSpec(memory_space=pltpu.VMEM)
    anywhere = pl.BlockSpec(memory_space=pl.ANY)
    shapes = (
        jax.ShapeDtypeStruct(m_unit, BF16),
        jax.ShapeDtypeStruct((BOTH, INNER_DEV), BF16),
        jax.ShapeDtypeStruct(unit, BF16),
        jax.ShapeDtypeStruct(unit, BF16),
        jax.ShapeDtypeStruct((WIDTH // 2, INNER_DEV), F32),
    )
    results = pl.pallas_call(
        layer_kernel,
        out_shape=shapes,
        in_specs=[pl.BlockSpec(memory_space=pltpu.SMEM), whole] + [anywhere] * 4,
        out_specs=(whole,) * 5,
        scratch_shapes=scratch,
        compiler_params=pltpu.CompilerParams(
            collective_id=0, has_side_effects=True, vmem_limit_bytes=63 * 2**20
        ),
    )(block_order, queries.reshape(BOTH, INNER_DEV), keys, values, out_weight, out_grad)
    mixed, query_grad, key_grad, value_grad, weight_grad = pl.pallas_call(
        results_kernel,
        out_shape=shapes,
        in_specs=[whole] * 5,
        out_specs=(anywhere,) * 5,
        scratch_shapes=[pltpu.SemaphoreType.DMA((5,))],
    )(*results)
    return (mixed, query_grad.reshape(unit), key_grad, value_grad, weight_grad.T)


def solution(mesh):
    return jax.shard_map(
        local,
        mesh=mesh,
        in_specs=(
            P(None, "seq", "tp"),
            P(None, "seq", "tp"),
            P(None, "seq", "tp"),
            P("seq"),
            P("tp", None),
            P(None, "seq", "tp"),
        ),
        out_specs=(
            P(None, "seq", "tp"),
            P(None, "seq", "tp"),
            P(None, "seq", "tp"),
            P(None, "seq", "tp"),
            P("tp", "seq"),
        ),
        check_vma=False,
    )
```

```python
import functools
import math

import jax
import jax.numpy as jnp
from jax import lax
from jax.experimental import pallas as pl
from jax.experimental.pallas import tpu as pltpu
from jax.sharding import PartitionSpec as P

HEAD_SIZE = 128
BLOCK = 16
HEADS_DEV = 3
ROWS = 256
BOTH = 2 * ROWS
POS_ROWS = ROWS // BLOCK
INNER_DEV = HEADS_DEV * HEAD_SIZE
SPLIT = 192
WIDTH = 640
MESH = pl.DeviceIdType.MESH
F32 = jnp.float32
BF16 = jnp.bfloat16
MASKED = -1e30
LOWEST = -1e29
LOG2_SCALE = math.log2(math.e) / math.sqrt(HEAD_SIZE)
SCALE = 1.0 / math.sqrt(HEAD_SIZE)


def dot(a, b):
    return lax.dot_general(a, b, (((1,), (0,)), ((), ())), preferred_element_type=F32)


def dot_nt(a, b):
    return lax.dot_general(a, b, (((1,), (1,)), ((), ())), preferred_element_type=F32)


def dot_tn(a, b):
    return lax.dot_general(a, b, (((0,), (0,)), ((), ())), preferred_element_type=F32)


def remote(src, dst, send_sem, recv_sem, device):
    return pltpu.make_async_remote_copy(
        src_ref=src,
        dst_ref=dst,
        send_sem=send_sem,
        recv_sem=recv_sem,
        device_id=device,
        device_id_type=MESH,
    )


def equal(a, n):
    return (a + 16 - n) // 16 - (a + 15 - n) // 16


class RingReduce:
    def __init__(self, piece, via, ring, cross, send, recv, plus, minus, partner):
        self.piece, self.via, self.ring, self.cross = piece, via, ring, cross
        self.send, self.recv = send, recv
        self.plus, self.minus, self.partner = plus, minus, partner

    def copy(self, kind, p, n):
        if kind == "cross":
            return remote(
                self.piece(1, 0), self.cross, self.send.at[12], self.recv.at[12], self.partner
            )
        at = 6 * p + 2 * ("far", "near", "joint").index(kind) + n
        half = 1 - n if kind == "near" else n
        source = self.piece(p, 2 if kind == "far" else (1, 3)[n]).at[half]
        target = self.via.at[p, n] if kind == "far" else self.ring.at[p, n, half]
        device = (self.plus, self.minus)[n]
        return remote(source, target, self.send.at[at], self.recv.at[at], device)

    def start(self, kind, p, which=(0, 1)):
        for n in which:
            self.copy(kind, p, n).start()

    def join(self, p, which=(0, 1)):
        for n in which:
            self.copy("far", p, n).wait_recv()
            target = self.piece(p, (1, 3)[n])
            target[n] = (target[n].astype(F32) + self.via[p, n].astype(F32)).astype(BF16)
            self.copy("joint", p, n).start()

    def gathered(self, p):
        for kind in ("near", "joint"):
            for n in (0, 1):
                self.copy(kind, p, n).wait_recv()
        own = self.piece(p, 0)
        return own[...].astype(F32) + self.ring[p, 0].astype(F32) + self.ring[p, 1].astype(F32)

    def to_partner(self):
        total = self.gathered(1)
        self.piece(1, 0)[...] = total.astype(BF16)
        self.copy("cross", 1, 0).start()

    def result(self):
        total = self.gathered(0)
        self.copy("cross", 1, 0).wait_recv()
        return total + self.cross[...].astype(F32)

    def finish(self, sides=(0, 1)):
        for p in sides:
            for kind in ("far", "near", "joint"):
                for n in (0, 1):
                    self.copy(kind, p, n).wait_send()
        if 1 in sides:
            self.copy("cross", 1, 0).wait_send()


def layer_kernel(
    order_ref, q_ref, k_ref, v_ref, weight_ref, og_ref,
    mixed_ref, qg_ref, kg_ref, vg_ref, wg_ref,
    kv, noisy_kv, w_ref, og, limit, qt, acc, stat, att_t, att, bias, head_t, head, dq,
    mixp, m_via, m_ring, m_cross,
    w_pair, w_out, w_recv, w_x, w_via, w_ring, w_final, w_turn,
    t_out, t_recv, t_mine, t_via, t_ring, t_cross,
    load, kv_send, kv_recv, og_send, og_recv,
    m_send, m_rsem, w_send, w_rsem, ws_send, ws_recv, wx_send, wx_recv, wf_sem,
    t_send, t_rsem, ts_send, ts_recv,
):
    s = lax.axis_index("seq")
    t = lax.axis_index("tp")
    y, x, c = s // 4, (s // 2) % 2, s % 2
    xh, z = t // 4, t % 4

    def slot(ys, xs, cs):
        return (ys * 2 + xs) * 2 + cs

    y_plus = {"seq": slot((y + 1) % 4, x, c)}
    y_minus = {"seq": slot((y + 3) % 4, x, c)}
    x_near = {"seq": slot(y, 1 - x, c)}
    sibling = {"seq": slot(y, x, 1 - c)}
    z_plus = {"tp": xh * 4 + (z + 1) % 4}
    z_minus = {"tp": xh * 4 + (z + 3) % 4}
    x_far = {"tp": (1 - xh) * 4 + z}

    barrier = pltpu.get_barrier_semaphore()
    partners = (y_plus, y_minus, x_near, sibling, z_plus, z_minus, x_far)
    for partner in partners:
        pl.semaphore_signal(barrier, inc=1, device_id=partner, device_id_type=MESH)

    loads = [
        pltpu.make_async_copy(src, dst, load.at[n])
        for n, (src, dst) in enumerate(
            (
                (k_ref.at[0], kv.at[s, 0, pl.ds(0, ROWS)]),
                (v_ref.at[0], kv.at[s, 1, pl.ds(0, ROWS)]),
                (og_ref, og.at[t]),
                (k_ref.at[1], noisy_kv.at[0]),
                (v_ref.at[1], noisy_kv.at[1]),
                (weight_ref, w_ref),
            )
        )
    ]
    for copy in loads:
        copy.start()

    mark_row = lax.broadcasted_iota(jnp.int32, (POS_ROWS, INNER_DEV), 0)
    lane = lax.broadcasted_iota(jnp.int32, (8, BOTH), 1)
    lane_block = (lane % ROWS) // BLOCK
    marks = jnp.zeros((POS_ROWS, INNER_DEV), F32)
    start = jnp.zeros((8, BOTH), F32)
    for b in range(POS_ROWS):
        position = order_ref[b].astype(F32)
        marks = jnp.where(mark_row == b, position, marks)
        start = jnp.where(lane_block == b, position * float(BLOCK), start)
    kv[s, 0, ROWS:] = marks.astype(BF16)
    limit[...] = start + jnp.where(lane < ROWS, lane % BLOCK, -1).astype(F32)

    def kv_copy(place, half, sem, device):
        part = kv.at[place, half, pl.ds(0, ROWS if half else ROWS + POS_ROWS)]
        return remote(part, part, kv_send.at[sem], kv_recv.at[place, half], device)

    near_place = slot(y, 1 - x, c)

    def ring_place(p, off):
        return slot((y + off) % 4, (x + p) % 2, c)

    def own_copy(kind, half):
        at = {"sibling": 0, "x": 16, "plus": 18, "minus": 20}[kind] + half
        device = {"sibling": sibling, "x": x_near, "plus": y_plus, "minus": y_minus}[kind]
        return kv_copy(s, half, at, device)

    def near_copy(kind, half):
        at = {"plus": 22, "minus": 24}[kind] + half
        return kv_copy(near_place, half, at, {"plus": y_plus, "minus": y_minus}[kind])

    def pass_plus(p):
        return kv_copy(ring_place(p, 3), 0, 26 + 2 * p, y_plus)

    def pass_minus(p):
        return kv_copy(ring_place(p, 1), 1, 27 + 2 * p, y_minus)

    def og_copy(place, half, sem, device, part=None):
        rows = {None: pl.ds(0, ROWS), 0: pl.ds(0, SPLIT), 1: pl.ds(SPLIT, ROWS - SPLIT)}[part]
        piece = og.at[place, half, rows]
        recv = og_recv.at[place, half + (2 if part == 1 else 0)]
        return remote(piece, piece, og_send.at[sem], recv, device)

    far_place = (1 - xh) * 4 + z

    def og_own(kind, half):
        if kind == "far":
            return og_copy(t, half, half, x_far, 0)
        at = {"plus": 2, "minus": 4}[kind] + half
        return og_copy(t, half, at, {"plus": z_plus, "minus": z_minus}[kind])

    def og_far(kind, half):
        at = {"plus": 6, "minus": 8}[kind] + half
        return og_copy(far_place, half, at, {"plus": z_plus, "minus": z_minus}[kind], 0)

    def og_place(a, off):
        return ((xh + a) % 2) * 4 + (z + off) % 4

    def og_pass_plus(a):
        return og_copy(og_place(a, 3), 0, 10 + 2 * a, z_plus, 0 if a else None)

    def og_pass_minus(a):
        return og_copy(og_place(a, 1), 1, 11 + 2 * a, z_minus, 0 if a else None)

    def og_late(off, half):
        return og_copy(og_place(0, off), half, 14 + 2 * off + half, x_far, 1)

    def og_wait(place, halves=(0, 1), part=None):
        for half in halves:
            og_copy(place, half, 0, z_plus, part).wait_recv()

    loads[0].wait()
    loads[1].wait()
    loads[2].wait()
    pl.semaphore_wait(barrier, len(partners))
    for n in (0, 1):
        own_copy("x", n).start()
        own_copy("plus", n).start()
        own_copy("minus", 1 - n).start()
    for n in (0, 1):
        og_own("plus", n).start()
        og_own("minus", 1 - n).start()
        og_own("far", n).start()
        own_copy("sibling", n).start()
    for n in (0, 1):
        og_late(0, n).start()

    for h in range(HEADS_DEV):
        cols = slice(h * HEAD_SIZE, (h + 1) * HEAD_SIZE)
        scaled = q_ref[:, cols].astype(F32).T * LOG2_SCALE
        high = scaled.astype(BF16)
        qt[h, :HEAD_SIZE] = high
        qt[h, HEAD_SIZE:] = (scaled - high.astype(F32)).astype(BF16)

    def cols_of(h):
        return slice(h * HEAD_SIZE, (h + 1) * HEAD_SIZE)

    def scores_of(key, h, first):
        return dot(jnp.concatenate([key, key], axis=1), qt[h, :, first:])

    loads[3].wait()
    loads[4].wait()
    row_block = lax.broadcasted_iota(jnp.int32, (ROWS, ROWS), 0) // BLOCK
    col_block = lax.broadcasted_iota(jnp.int32, (ROWS, ROWS), 1) // BLOCK
    self_bias = jnp.where(row_block == col_block, 0.0, MASKED).astype(F32)
    bias[:, :ROWS] = self_bias

    for h in range(HEADS_DEV):
        scores = scores_of(noisy_kv[0, :, cols_of(h)], h, ROWS) + bias[:, :ROWS]
        top = jnp.max(scores, axis=0, keepdims=True)
        weights = jnp.exp2(scores - top)
        stat[0, h : h + 1, :ROWS] = jnp.full((1, ROWS), LOWEST, F32)
        stat[0, h : h + 1, ROWS:] = top
        stat[1, h : h + 1, :ROWS] = jnp.zeros((1, ROWS), F32)
        stat[1, h : h + 1, ROWS:] = jnp.sum(weights, axis=0, keepdims=True)
        acc[cols_of(h), :ROWS] = jnp.zeros((HEAD_SIZE, ROWS), F32)
        acc[cols_of(h), ROWS:] = dot_tn(noisy_kv[1, :, cols_of(h)], weights.astype(BF16))

    def set_bias(place):
        position = kv[place, 0, ROWS:, :HEAD_SIZE].astype(F32)
        offset = lax.broadcasted_iota(jnp.int32, (BLOCK, HEAD_SIZE), 0).astype(F32)
        for b in range(POS_ROWS):
            code = position[b : b + 1] * float(BLOCK) + offset
            for n in range(BOTH // HEAD_SIZE):
                lanes = slice(n * HEAD_SIZE, (n + 1) * HEAD_SIZE)
                bias[b * BLOCK : (b + 1) * BLOCK, lanes] = jnp.where(
                    code <= limit[0:1, lanes], 0.0, MASKED
                ).astype(F32)

    def columns(j):
        return pl.ds(pl.multiple_of(j * WIDTH, HEAD_SIZE), WIDTH)

    half_rows = INNER_DEV // 2
    head_t[...] = jnp.zeros((INNER_DEV, BOTH), F32)

    loads[5].wait()

    og_order = ((0, 0), (0, 3), (0, 1), (1, 0), (0, 2), (1, 3), (1, 1), (1, 2))

    def og_at(k):
        a = sum(u[0] * equal(k, n) for n, u in enumerate(og_order))
        off = sum(u[1] * equal(k, n) for n, u in enumerate(og_order))
        return og_place(a, off)

    def head_step(k, carry):
        j = og_at(k)
        head_t[...] += dot_nt(w_ref[:, columns(j)], og[j].reshape(BOTH, WIDTH))
        return carry

    def forward_step(i, carry):
        n, d = i // 2, i % 2
        p = n // 5 + (n + 6) // 7 - (n + 5) // 7
        m = (n + 1) % 3
        off = ((n + 6) // 8) * (m + 3 * ((2 - m) // 2))
        place = slot((y + off) % 4, (x + p) % 2, (c + d) % 2)

        @pl.when(i == 6)
        def _():
            og_wait(og_place(0, 3), (0,))
            og_pass_plus(0).start()
            og_wait(og_place(0, 1), (1,))
            og_pass_minus(0).start()

        @pl.when(i == 8)
        def _():
            og_wait(far_place, (0,), 0)
            og_far("plus", 0).start()
            og_wait(og_place(0, 3), (1,))
            og_wait(og_place(0, 1), (0,))
            for off in (3, 1):
                for half in (0, 1):
                    og_late(off, half).start()

        @pl.when(i == 12)
        def _():
            og_wait(og_place(0, 2))
            for half in (0, 1):
                og_late(2, half).start()

        @pl.when(i == 10)
        def _():
            og_wait(far_place, (1,), 0)
            og_far("minus", 1).start()
            og_far("plus", 1).start()
            og_far("minus", 0).start()

        @pl.when(i == 14)
        def _():
            og_wait(far_place, (0, 1), 1)
            lax.fori_loop(0, 5, head_step, 0)

        for half in (0, 1):

            @pl.when(i > 0)
            def _():
                kv_copy(place, half, 0, sibling).wait_recv()

            @pl.when(i == 2)
            def _():
                near_copy("plus", half).start()
                near_copy("minus", half).start()

            for side, at in ((0, 4), (1, 10)):

                @pl.when(i == at + 2 * half)
                def _():
                    (pass_minus if half else pass_plus)(side).start()

            @pl.when((i > 0) & (d == 0))
            def _():
                kv_copy(place, half, 2 * n + half, sibling).start()

        set_bias(place)
        for h in range(HEADS_DEV):
            scores = scores_of(kv[place, 0, :ROWS, cols_of(h)], h, 0) + bias[...]
            old = stat[0, h : h + 1]
            top = jnp.maximum(old, jnp.max(scores, axis=0, keepdims=True))
            weights = jnp.exp2(scores - top)
            factor = jnp.exp2(old - top)
            stat[0, h : h + 1] = top
            stat[1, h : h + 1] = stat[1, h : h + 1] * factor + jnp.sum(
                weights, axis=0, keepdims=True
            )
            acc[cols_of(h)] = acc[cols_of(h)] * factor + dot_tn(
                kv[place, 1, :ROWS, cols_of(h)], weights.astype(BF16)
            )
        return carry

    lax.fori_loop(0, 16, forward_step, 0)
    og_wait(og_place(1, 3), (0,), 0)
    og_pass_plus(1).start()
    og_wait(og_place(1, 1), (1,), 0)
    og_pass_minus(1).start()

    for h in range(HEADS_DEV):
        total = stat[1, h : h + 1]
        out = acc[cols_of(h)] / total
        att_t[cols_of(h)] = out.astype(BF16)
        att[:, cols_of(h)] = out.T.astype(BF16)
        stat[0, h : h + 1] = stat[0, h : h + 1] + jnp.log2(total)

    def mix_step(side, n, carry):
        j = side * 4 + n
        mixp[j] = dot(att[...], w_ref[:, columns(j)]).astype(BF16).reshape(2, ROWS, WIDTH)
        return carry

    def w_copy(j):
        return remote(w_out.at[j], w_recv.at[j], ws_send.at[j], ws_recv.at[j], sibling)

    def w_across(n):
        return remote(w_pair.at[2 * n + 1 - x], w_x.at[n], wx_send.at[n], wx_recv.at[n], x_near)

    def w_sum(j):
        w_copy(j).wait_recv()
        w_pair[j] = (w_pair[j].astype(F32) + w_recv[j].astype(F32)).astype(BF16)

        @pl.when(j % 2 == 1 - x)
        def _():
            w_across(j // 2).start()

    def projection_step(k, carry):
        j = og_at(k)

        for half, pieces in enumerate(((6, 7), (5, 7))):
            for n in pieces:

                @pl.when(k == n)
                def _():
                    og_wait(j, (half,), 0)

        @pl.when(k > 4)
        def _():
            og_wait(j, (0, 1), 1)
            head_step(k, 0)

        grads = og[j].reshape(BOTH, WIDTH)
        theirs = att_t[pl.ds(pl.multiple_of((1 - c) * half_rows, 16), half_rows)]
        w_out[j] = dot(theirs, grads).astype(BF16).reshape(2, half_rows // 2, WIDTH)
        w_copy(j).start()
        mine = att_t[pl.ds(pl.multiple_of(c * half_rows, 16), half_rows)]
        w_pair[j] = dot(mine, grads).astype(BF16).reshape(2, half_rows // 2, WIDTH)

        @pl.when(k > 0)
        def _():
            w_sum(og_at(k - 1))

        return carry

    mix = RingReduce(
        lambda p, r: mixp.at[og_place(p, r)], m_via, m_ring, m_cross, m_send, m_rsem,
        z_plus, z_minus, x_far,
    )
    weight = RingReduce(
        lambda p, r: w_pair.at[((y + r) % 4) * 2 + (x + p) % 2], w_via, w_ring, None,
        w_send, w_rsem, y_plus, y_minus, x_near,
    )
    lax.fori_loop(0, 5, projection_step, 0)
    lax.fori_loop(0, 4, functools.partial(mix_step, 1 - xh), 0)
    mix.start("far", 1)
    mix.start("near", 1)
    lax.fori_loop(5, 7, projection_step, 0)
    lax.fori_loop(0, 4, functools.partial(mix_step, xh), 0)
    lax.fori_loop(7, 8, projection_step, 0)
    w_sum(og_at(7))

    turns = [(1, 2), (0, 2), (1, 1), (1, 3), (0, 1), (0, 3), (1, 0), (0, 0)]
    term = RingReduce(
        lambda p, r: t_recv.at[turns.index((p, r))], t_via, t_ring, t_cross,
        t_send, t_rsem, y_plus, y_minus, x_near,
    )

    for h in range(HEADS_DEV):
        grad = head_t[cols_of(h)]
        rounded = grad.astype(BF16)
        head[:, cols_of(h)] = grad.T.astype(BF16)
        stat[1, h : h + 1] = jnp.sum(
            rounded.astype(F32) * att_t[cols_of(h)].astype(F32), axis=0, keepdims=True
        )
        att_t[cols_of(h)] = rounded
        dq[cols_of(h)] = jnp.zeros((HEAD_SIZE, BOTH), F32)
    head_tb = att_t

    def backward_tile(key, value, h, first, masks):
        scores = scores_of(key, h, first) + masks
        probs = jnp.exp2(scores - stat[0, h : h + 1, first:])
        value_term = dot(probs.astype(BF16), head[first:, cols_of(h)])
        prob_grad = dot(value, head_tb[cols_of(h), first:])
        score_grad = (probs * (prob_grad - stat[1, h : h + 1, first:])).astype(BF16)
        key_term = dot(score_grad, q_ref[first:, cols_of(h)]) * SCALE
        dq[cols_of(h), first:] += dot_tn(key, score_grad)
        return key_term.astype(BF16), value_term.astype(BF16)

    def t_copy(j):
        return remote(t_out.at[j], t_recv.at[j], ts_send.at[j], ts_recv.at[j], sibling)

    w_mine = pl.multiple_of(c * half_rows, 16)

    def final_copy():
        part = w_final.at[pl.ds(w_mine, half_rows)]
        return remote(part, part, wf_sem.at[0], wf_sem.at[1], sibling)

    def backward_step(i, carry):
        odd, last, second = i % 2, equal(i, 15), equal(i, 1)
        late = (i + 13) // 16
        d = 1 - ((1 - odd) * late + last + second)
        j = late * (odd * ((i + 1) // 2) + (1 - odd) * (i // 2 - 1) - last) + equal(i, 2)
        p = sum(turn[0] * equal(j, n) for n, turn in enumerate(turns))
        off = sum(turn[1] * equal(j, n) for n, turn in enumerate(turns))
        place = slot((y + off) % 4, (x + p) % 2, (c + d) % 2)

        @pl.when(i == 2)
        def _():
            mix.join(1)
            mix.start("far", 0)
            mix.start("near", 0)

        @pl.when(i == 13)
        def _():
            for n in range(4):
                w_across(n).wait_recv()
                mine = w_pair.at[2 * n + x]
                mine[...] = (mine[...].astype(F32) + w_x[n].astype(F32)).astype(BF16)
            weight.start("far", 0)
            weight.start("near", 0)

        @pl.when(i == 15)
        def _():
            term.to_partner()

        @pl.when(i == 11)
        def _():
            mix.to_partner()

        set_bias(place)
        for h in range(HEADS_DEV):
            key_term, value_term = backward_tile(
                kv[place, 0, :ROWS, cols_of(h)], kv[place, 1, :ROWS, cols_of(h)], h, 0, bias[...]
            )
            t_mine[0, :, cols_of(h)] = key_term
            t_mine[1, :, cols_of(h)] = value_term

        @pl.when(d == 1)
        def _():
            t_out[j] = t_mine[...]
            t_copy(j).start()

        @pl.when(d == 0)
        def _():
            t_copy(j).wait_recv()
            t_recv[j] = (t_recv[j].astype(F32) + t_mine[...].astype(F32)).astype(BF16)

        for n, (p_now, r) in enumerate(turns):
            if r == 0:
                continue

            @pl.when(i == (2 * n + 2 if n else 1))
            def _():
                if r == 2:
                    term.start("far", p_now)
                else:
                    which = (0,) if r == 1 else (1,)
                    term.start("near", p_now, which)
                    term.join(p_now, which)

        return carry

    lax.fori_loop(0, 16, backward_step, 0)

    mix.join(0)
    weight.join(0)
    bias[:, :ROWS] = self_bias
    for h in range(HEADS_DEV):
        key_term, value_term = backward_tile(
            noisy_kv[0, :, cols_of(h)], noisy_kv[1, :, cols_of(h)], h, ROWS, bias[:, :ROWS]
        )
        kg_ref[1, :, cols_of(h)] = key_term
        vg_ref[1, :, cols_of(h)] = value_term

    for h in range(HEADS_DEV):
        qg_ref[:, cols_of(h)] = (dq[cols_of(h)] * SCALE).T.astype(BF16)


    terms = term.result().astype(BF16)
    kg_ref[0] = terms[0]
    vg_ref[0] = terms[1]

    w_final[pl.ds(w_mine, half_rows)] = weight.gathered(0).reshape(half_rows, WIDTH)
    final_copy().start()
    mixed_ref[...] = mix.result().astype(BF16)

    w_theirs = pl.multiple_of((1 - c) * half_rows, 16)
    part = w_final.at[pl.ds(w_theirs, half_rows)]
    remote(part, part, wf_sem.at[0], wf_sem.at[1], sibling).wait_recv()
    for n in range(INNER_DEV // HEAD_SIZE):
        w_turn[:, cols_of(n)] = w_final[cols_of(n)].T
    wg_ref[...] = w_turn[pl.ds(pl.multiple_of(c * (WIDTH // 2), 8), WIDTH // 2)]

    for half in (0, 1):
        for kind in ("x", "plus", "minus"):
            own_copy(kind, half).wait_send()
        for kind in ("plus", "minus"):
            near_copy(kind, half).wait_send()
            og_own(kind, half).wait_send()
            og_far(kind, half).wait_send()
        for off in range(4):
            og_late(off, half).wait_send()
        og_own("far", half).wait_send()
        for n in range(8):
            kv_copy(s, half, 2 * n + half, sibling).wait_send()
    for n in range(8):
        w_copy(n).wait_send()
        t_copy(n).wait_send()
    for n in range(4):
        w_across(n).wait_send()
    for p in (0, 1):
        pass_plus(p).wait_send()
        pass_minus(p).wait_send()
        og_pass_plus(p).wait_send()
        og_pass_minus(p).wait_send()
    mix.finish()
    weight.finish((0,))
    term.finish()
    final_copy().wait_send()


def results_kernel(*refs):
    count = len(refs) // 2
    copies = [
        pltpu.make_async_copy(refs[n], refs[count + n], refs[-1].at[n]) for n in range(count)
    ]
    for copy in copies:
        copy.start()
    for copy in copies:
        copy.wait()


def local(queries, keys, values, block_order, out_weight, out_grad):
    unit = (2, ROWS, INNER_DEV)
    w_unit = (2, INNER_DEV // 4, WIDTH)
    m_unit = (2, ROWS, WIDTH)

    def buffer(*shape, dtype=BF16):
        return pltpu.VMEM(shape, dtype)

    def sums(u):
        return [buffer(2, *u), buffer(2, 2, *u), buffer(*u)]

    scratch = [
        buffer(16, 2, ROWS + POS_ROWS, INNER_DEV),
        buffer(*unit),
        buffer(*out_weight.shape),
        buffer(8, *m_unit),
        buffer(8, BOTH, dtype=F32),
        buffer(HEADS_DEV, 2 * HEAD_SIZE, BOTH),
        buffer(INNER_DEV, BOTH, dtype=F32),
        buffer(2, 8, BOTH, dtype=F32),
        buffer(INNER_DEV, BOTH),
        buffer(BOTH, INNER_DEV),
        buffer(ROWS, BOTH, dtype=F32),
        buffer(INNER_DEV, BOTH, dtype=F32),
        buffer(BOTH, INNER_DEV),
        buffer(INNER_DEV, BOTH, dtype=F32),
        buffer(8, *m_unit), *sums(m_unit),
        buffer(8, *w_unit), buffer(8, *w_unit), buffer(8, *w_unit), buffer(4, *w_unit),
        *sums(w_unit)[:2], buffer(INNER_DEV, WIDTH, dtype=F32),
        buffer(WIDTH, INNER_DEV, dtype=F32),
        buffer(8, *unit), buffer(8, *unit), buffer(*unit), *sums(unit),
        *(
            pltpu.SemaphoreType.DMA(shape)
            for shape in (
                (6,), (30,), (16, 2), (22,), (8, 4), (13,), (13,), (13,), (13,),
                (8,), (8,), (4,), (4,), (2,), (13,), (13,), (8,), (8,),
            )
        ),
    ]
    whole = pl.BlockSpec(memory_space=pltpu.VMEM)
    anywhere = pl.BlockSpec(memory_space=pl.ANY)
    shapes = (
        jax.ShapeDtypeStruct(m_unit, BF16),
        jax.ShapeDtypeStruct((BOTH, INNER_DEV), BF16),
        jax.ShapeDtypeStruct(unit, BF16),
        jax.ShapeDtypeStruct(unit, BF16),
        jax.ShapeDtypeStruct((WIDTH // 2, INNER_DEV), F32),
    )
    results = pl.pallas_call(
        layer_kernel,
        out_shape=shapes,
        in_specs=[pl.BlockSpec(memory_space=pltpu.SMEM), whole] + [anywhere] * 4,
        out_specs=(whole,) * 5,
        scratch_shapes=scratch,
        compiler_params=pltpu.CompilerParams(
            collective_id=0, has_side_effects=True, vmem_limit_bytes=63 * 2**20
        ),
    )(block_order, queries.reshape(BOTH, INNER_DEV), keys, values, out_weight, out_grad)
    mixed, query_grad, key_grad, value_grad, weight_grad = pl.pallas_call(
        results_kernel,
        out_shape=shapes,
        in_specs=[whole] * 5,
        out_specs=(anywhere,) * 5,
        scratch_shapes=[pltpu.SemaphoreType.DMA((5,))],
    )(*results)
    return (mixed, query_grad.reshape(unit), key_grad, value_grad, weight_grad.T)


def solution(mesh):
    return jax.shard_map(
        local,
        mesh=mesh,
        in_specs=(
            P(None, "seq", "tp"),
            P(None, "seq", "tp"),
            P(None, "seq", "tp"),
            P("seq"),
            P("tp", None),
            P(None, "seq", "tp"),
        ),
        out_specs=(
            P(None, "seq", "tp"),
            P(None, "seq", "tp"),
            P(None, "seq", "tp"),
            P(None, "seq", "tp"),
            P("tp", "seq"),
        ),
        check_vma=False,
    )
```

```python
import functools
import math

import jax
import jax.numpy as jnp
from jax import lax
from jax.experimental import pallas as pl
from jax.experimental.pallas import tpu as pltpu
from jax.sharding import PartitionSpec as P

HEAD_SIZE = 128
BLOCK = 16
HEADS_DEV = 3
ROWS = 256
BOTH = 2 * ROWS
POS_ROWS = ROWS // BLOCK
INNER_DEV = HEADS_DEV * HEAD_SIZE
SPLIT = 192
WIDTH = 640
MESH = pl.DeviceIdType.MESH
F32 = jnp.float32
BF16 = jnp.bfloat16
MASKED = -1e30
LOWEST = -1e29
LOG2_SCALE = math.log2(math.e) / math.sqrt(HEAD_SIZE)
SCALE = 1.0 / math.sqrt(HEAD_SIZE)


def dot(a, b):
    return lax.dot_general(a, b, (((1,), (0,)), ((), ())), preferred_element_type=F32)


def dot_nt(a, b):
    return lax.dot_general(a, b, (((1,), (1,)), ((), ())), preferred_element_type=F32)


def dot_tn(a, b):
    return lax.dot_general(a, b, (((0,), (0,)), ((), ())), preferred_element_type=F32)


def remote(src, dst, send_sem, recv_sem, device):
    return pltpu.make_async_remote_copy(
        src_ref=src,
        dst_ref=dst,
        send_sem=send_sem,
        recv_sem=recv_sem,
        device_id=device,
        device_id_type=MESH,
    )


def equal(a, n):
    return (a + 16 - n) // 16 - (a + 15 - n) // 16


class RingReduce:
    def __init__(self, piece, via, ring, cross, send, recv, plus, minus, partner):
        self.piece, self.via, self.ring, self.cross = piece, via, ring, cross
        self.send, self.recv = send, recv
        self.plus, self.minus, self.partner = plus, minus, partner

    def copy(self, kind, p, n):
        if kind == "cross":
            return remote(
                self.piece(1, 0), self.cross, self.send.at[12], self.recv.at[12], self.partner
            )
        at = 6 * p + 2 * ("far", "near", "joint").index(kind) + n
        half = 1 - n if kind == "near" else n
        source = self.piece(p, 2 if kind == "far" else (1, 3)[n]).at[half]
        target = self.via.at[p, n] if kind == "far" else self.ring.at[p, n, half]
        device = (self.plus, self.minus)[n]
        return remote(source, target, self.send.at[at], self.recv.at[at], device)

    def start(self, kind, p, which=(0, 1)):
        for n in which:
            self.copy(kind, p, n).start()

    def join(self, p, which=(0, 1)):
        for n in which:
            self.copy("far", p, n).wait_recv()
            target = self.piece(p, (1, 3)[n])
            target[n] = (target[n].astype(F32) + self.via[p, n].astype(F32)).astype(BF16)
            self.copy("joint", p, n).start()

    def gathered(self, p):
        for kind in ("near", "joint"):
            for n in (0, 1):
                self.copy(kind, p, n).wait_recv()
        own = self.piece(p, 0)
        return own[...].astype(F32) + self.ring[p, 0].astype(F32) + self.ring[p, 1].astype(F32)

    def to_partner(self):
        total = self.gathered(1)
        self.piece(1, 0)[...] = total.astype(BF16)
        self.copy("cross", 1, 0).start()

    def result(self):
        total = self.gathered(0)
        self.copy("cross", 1, 0).wait_recv()
        return total + self.cross[...].astype(F32)

    def finish(self, sides=(0, 1)):
        for p in sides:
            for kind in ("far", "near", "joint"):
                for n in (0, 1):
                    self.copy(kind, p, n).wait_send()
        if 1 in sides:
            self.copy("cross", 1, 0).wait_send()


def layer_kernel(
    order_ref, q_in, k_ref, v_ref, weight_ref, og_ref,
    mixed_ref, qg_ref, kg_ref, vg_ref, wg_ref,
    kv, noisy_kv, w_ref, q_ref, og, limit, qt, acc, stat, att_t, att, bias, head_t, head, dq,
    mixp, m_via, m_ring, m_cross,
    w_pair, w_out, w_recv, w_x, w_via, w_ring, w_final, w_turn,
    t_out, t_recv, t_mine, t_via, t_ring, t_cross,
    load, kv_send, kv_recv, og_send, og_recv,
    m_send, m_rsem, w_send, w_rsem, ws_send, ws_recv, wx_send, wx_recv, wf_sem,
    t_send, t_rsem, ts_send, ts_recv,
):
    s = lax.axis_index("seq")
    t = lax.axis_index("tp")
    y, x, c = s // 4, (s // 2) % 2, s % 2
    xh, z = t // 4, t % 4

    def slot(ys, xs, cs):
        return (ys * 2 + xs) * 2 + cs

    y_plus = {"seq": slot((y + 1) % 4, x, c)}
    y_minus = {"seq": slot((y + 3) % 4, x, c)}
    x_near = {"seq": slot(y, 1 - x, c)}
    sibling = {"seq": slot(y, x, 1 - c)}
    z_plus = {"tp": xh * 4 + (z + 1) % 4}
    z_minus = {"tp": xh * 4 + (z + 3) % 4}
    x_far = {"tp": (1 - xh) * 4 + z}

    barrier = pltpu.get_barrier_semaphore()
    partners = (y_plus, y_minus, x_near, sibling, z_plus, z_minus, x_far)
    for partner in partners:
        pl.semaphore_signal(barrier, inc=1, device_id=partner, device_id_type=MESH)

    loads = [
        pltpu.make_async_copy(src, dst, load.at[n])
        for n, (src, dst) in enumerate(
            (
                (k_ref.at[0], kv.at[s, 0, pl.ds(0, ROWS)]),
                (v_ref.at[0], kv.at[s, 1, pl.ds(0, ROWS)]),
                (og_ref, og.at[t]),
                (k_ref.at[1], noisy_kv.at[0]),
                (v_ref.at[1], noisy_kv.at[1]),
                (weight_ref, w_ref),
                (q_in, q_ref),
            )
        )
    ]
    for copy in loads[:3]:
        copy.start()

    mark_row = lax.broadcasted_iota(jnp.int32, (POS_ROWS, INNER_DEV), 0)
    lane = lax.broadcasted_iota(jnp.int32, (8, BOTH), 1)
    lane_block = (lane % ROWS) // BLOCK
    marks = jnp.zeros((POS_ROWS, INNER_DEV), F32)
    start = jnp.zeros((8, BOTH), F32)
    for b in range(POS_ROWS):
        position = order_ref[b].astype(F32)
        marks = jnp.where(mark_row == b, position, marks)
        start = jnp.where(lane_block == b, position * float(BLOCK), start)
    kv[s, 0, ROWS:] = marks.astype(BF16)
    limit[...] = start + jnp.where(lane < ROWS, lane % BLOCK, -1).astype(F32)

    def kv_copy(place, half, sem, device):
        part = kv.at[place, half, pl.ds(0, ROWS if half else ROWS + POS_ROWS)]
        return remote(part, part, kv_send.at[sem], kv_recv.at[place, half], device)

    near_place = slot(y, 1 - x, c)

    def ring_place(p, off):
        return slot((y + off) % 4, (x + p) % 2, c)

    def own_copy(kind, half):
        at = {"sibling": 0, "x": 16, "plus": 18, "minus": 20}[kind] + half
        device = {"sibling": sibling, "x": x_near, "plus": y_plus, "minus": y_minus}[kind]
        return kv_copy(s, half, at, device)

    def near_copy(kind, half):
        at = {"plus": 22, "minus": 24}[kind] + half
        return kv_copy(near_place, half, at, {"plus": y_plus, "minus": y_minus}[kind])

    def pass_plus(p):
        return kv_copy(ring_place(p, 3), 0, 26 + 2 * p, y_plus)

    def pass_minus(p):
        return kv_copy(ring_place(p, 1), 1, 27 + 2 * p, y_minus)

    def og_copy(place, half, sem, device, part=None):
        rows = {None: pl.ds(0, ROWS), 0: pl.ds(0, SPLIT), 1: pl.ds(SPLIT, ROWS - SPLIT)}[part]
        piece = og.at[place, half, rows]
        recv = og_recv.at[place, half + (2 if part == 1 else 0)]
        return remote(piece, piece, og_send.at[sem], recv, device)

    far_place = (1 - xh) * 4 + z

    def og_own(kind, half):
        if kind == "far":
            return og_copy(t, half, half, x_far, 0)
        at = {"plus": 2, "minus": 4}[kind] + half
        return og_copy(t, half, at, {"plus": z_plus, "minus": z_minus}[kind])

    def og_far(kind, half):
        at = {"plus": 6, "minus": 8}[kind] + half
        return og_copy(far_place, half, at, {"plus": z_plus, "minus": z_minus}[kind], 0)

    def og_place(a, off):
        return ((xh + a) % 2) * 4 + (z + off) % 4

    def og_pass_plus(a):
        return og_copy(og_place(a, 3), 0, 10 + 2 * a, z_plus, 0 if a else None)

    def og_pass_minus(a):
        return og_copy(og_place(a, 1), 1, 11 + 2 * a, z_minus, 0 if a else None)

    def og_late(off, half):
        return og_copy(og_place(0, off), half, 14 + 2 * off + half, x_far, 1)

    def og_wait(place, halves=(0, 1), part=None):
        for half in halves:
            og_copy(place, half, 0, z_plus, part).wait_recv()

    loads[0].wait()
    loads[1].wait()
    loads[2].wait()
    pl.semaphore_wait(barrier, len(partners))
    for n in (0, 1):
        own_copy("x", n).start()
        own_copy("plus", n).start()
        own_copy("minus", 1 - n).start()
    for n in (0, 1):
        og_own("plus", n).start()
        og_own("minus", 1 - n).start()
        og_own("far", n).start()
        own_copy("sibling", n).start()
    for n in (0, 1):
        og_late(0, n).start()
    for n in (6, 3, 4, 5):
        loads[n].start()
    loads[6].wait()

    for h in range(HEADS_DEV):
        cols = slice(h * HEAD_SIZE, (h + 1) * HEAD_SIZE)
        scaled = q_ref[:, cols].astype(F32).T * LOG2_SCALE
        high = scaled.astype(BF16)
        qt[h, :HEAD_SIZE] = high
        qt[h, HEAD_SIZE:] = (scaled - high.astype(F32)).astype(BF16)

    def cols_of(h):
        return slice(h * HEAD_SIZE, (h + 1) * HEAD_SIZE)

    def scores_of(key, h, first):
        return dot(jnp.concatenate([key, key], axis=1), qt[h, :, first:])

    loads[3].wait()
    loads[4].wait()
    row_block = lax.broadcasted_iota(jnp.int32, (ROWS, ROWS), 0) // BLOCK
    col_block = lax.broadcasted_iota(jnp.int32, (ROWS, ROWS), 1) // BLOCK
    self_bias = jnp.where(row_block == col_block, 0.0, MASKED).astype(F32)
    bias[:, :ROWS] = self_bias

    for h in range(HEADS_DEV):
        scores = scores_of(noisy_kv[0, :, cols_of(h)], h, ROWS) + bias[:, :ROWS]
        top = jnp.max(scores, axis=0, keepdims=True)
        weights = jnp.exp2(scores - top)
        stat[0, h : h + 1, :ROWS] = jnp.full((1, ROWS), LOWEST, F32)
        stat[0, h : h + 1, ROWS:] = top
        stat[1, h : h + 1, :ROWS] = jnp.zeros((1, ROWS), F32)
        stat[1, h : h + 1, ROWS:] = jnp.sum(weights, axis=0, keepdims=True)
        acc[cols_of(h), :ROWS] = jnp.zeros((HEAD_SIZE, ROWS), F32)
        acc[cols_of(h), ROWS:] = dot_tn(noisy_kv[1, :, cols_of(h)], weights.astype(BF16))

    def set_bias(place):
        position = kv[place, 0, ROWS:, :HEAD_SIZE].astype(F32)
        offset = lax.broadcasted_iota(jnp.int32, (BLOCK, HEAD_SIZE), 0).astype(F32)
        for b in range(POS_ROWS):
            code = position[b : b + 1] * float(BLOCK) + offset
            for n in range(BOTH // HEAD_SIZE):
                lanes = slice(n * HEAD_SIZE, (n + 1) * HEAD_SIZE)
                bias[b * BLOCK : (b + 1) * BLOCK, lanes] = jnp.where(
                    code <= limit[0:1, lanes], 0.0, MASKED
                ).astype(F32)

    def columns(j):
        return pl.ds(pl.multiple_of(j * WIDTH, HEAD_SIZE), WIDTH)

    half_rows = INNER_DEV // 2
    head_t[...] = jnp.zeros((INNER_DEV, BOTH), F32)

    loads[5].wait()

    og_order = ((0, 0), (0, 3), (0, 1), (1, 0), (0, 2), (1, 3), (1, 1), (1, 2))

    def og_at(k):
        a = sum(u[0] * equal(k, n) for n, u in enumerate(og_order))
        off = sum(u[1] * equal(k, n) for n, u in enumerate(og_order))
        return og_place(a, off)

    def head_step(k, carry):
        j = og_at(k)
        head_t[...] += dot_nt(w_ref[:, columns(j)], og[j].reshape(BOTH, WIDTH))
        return carry

    def forward_step(i, carry):
        n, d = i // 2, i % 2
        p = n // 5 + (n + 6) // 7 - (n + 5) // 7
        m = (n + 1) % 3
        off = ((n + 6) // 8) * (m + 3 * ((2 - m) // 2))
        place = slot((y + off) % 4, (x + p) % 2, (c + d) % 2)

        @pl.when(i == 6)
        def _():
            og_wait(og_place(0, 3), (0,))
            og_pass_plus(0).start()
            og_wait(og_place(0, 1), (1,))
            og_pass_minus(0).start()

        @pl.when(i == 8)
        def _():
            og_wait(far_place, (0,), 0)
            og_far("plus", 0).start()
            og_wait(og_place(0, 3), (1,))
            og_wait(og_place(0, 1), (0,))
            for off in (3, 1):
                for half in (0, 1):
                    og_late(off, half).start()

        @pl.when(i == 12)
        def _():
            og_wait(og_place(0, 2))
            for half in (0, 1):
                og_late(2, half).start()

        @pl.when(i == 10)
        def _():
            og_wait(far_place, (1,), 0)
            og_far("minus", 1).start()
            og_far("plus", 1).start()
            og_far("minus", 0).start()

        @pl.when(i == 14)
        def _():
            og_wait(far_place, (0, 1), 1)
            lax.fori_loop(0, 5, head_step, 0)

        for half in (0, 1):

            @pl.when(i > 0)
            def _():
                kv_copy(place, half, 0, sibling).wait_recv()

            @pl.when(i == 2)
            def _():
                near_copy("plus", half).start()
                near_copy("minus", half).start()

            for side, at in ((0, 4), (1, 10)):

                @pl.when(i == at + 2 * half)
                def _():
                    (pass_minus if half else pass_plus)(side).start()

            @pl.when((i > 0) & (d == 0))
            def _():
                kv_copy(place, half, 2 * n + half, sibling).start()

        set_bias(place)
        for h in range(HEADS_DEV):
            scores = scores_of(kv[place, 0, :ROWS, cols_of(h)], h, 0) + bias[...]
            old = stat[0, h : h + 1]
            top = jnp.maximum(old, jnp.max(scores, axis=0, keepdims=True))
            weights = jnp.exp2(scores - top)
            factor = jnp.exp2(old - top)
            stat[0, h : h + 1] = top
            stat[1, h : h + 1] = stat[1, h : h + 1] * factor + jnp.sum(
                weights, axis=0, keepdims=True
            )
            acc[cols_of(h)] = acc[cols_of(h)] * factor + dot_tn(
                kv[place, 1, :ROWS, cols_of(h)], weights.astype(BF16)
            )
        return carry

    lax.fori_loop(0, 16, forward_step, 0)
    og_wait(og_place(1, 3), (0,), 0)
    og_pass_plus(1).start()
    og_wait(og_place(1, 1), (1,), 0)
    og_pass_minus(1).start()

    for h in range(HEADS_DEV):
        total = stat[1, h : h + 1]
        out = acc[cols_of(h)] / total
        att_t[cols_of(h)] = out.astype(BF16)
        att[:, cols_of(h)] = out.T.astype(BF16)
        stat[0, h : h + 1] = stat[0, h : h + 1] + jnp.log2(total)

    def mix_step(side, n, carry):
        j = side * 4 + n
        mixp[j] = dot(att[...], w_ref[:, columns(j)]).astype(BF16).reshape(2, ROWS, WIDTH)
        return carry

    def w_copy(j):
        return remote(w_out.at[j], w_recv.at[j], ws_send.at[j], ws_recv.at[j], sibling)

    def w_across(n):
        return remote(w_pair.at[2 * n + 1 - x], w_x.at[n], wx_send.at[n], wx_recv.at[n], x_near)

    def w_sum(j):
        w_copy(j).wait_recv()
        w_pair[j] = (w_pair[j].astype(F32) + w_recv[j].astype(F32)).astype(BF16)

        @pl.when(j % 2 == 1 - x)
        def _():
            w_across(j // 2).start()

    def projection_step(k, carry):
        j = og_at(k)

        for half, pieces in enumerate(((6, 7), (5, 7))):
            for n in pieces:

                @pl.when(k == n)
                def _():
                    og_wait(j, (half,), 0)

        @pl.when(k > 4)
        def _():
            og_wait(j, (0, 1), 1)
            head_step(k, 0)

        grads = og[j].reshape(BOTH, WIDTH)
        theirs = att_t[pl.ds(pl.multiple_of((1 - c) * half_rows, 16), half_rows)]
        w_out[j] = dot(theirs, grads).astype(BF16).reshape(2, half_rows // 2, WIDTH)
        w_copy(j).start()
        mine = att_t[pl.ds(pl.multiple_of(c * half_rows, 16), half_rows)]
        w_pair[j] = dot(mine, grads).astype(BF16).reshape(2, half_rows // 2, WIDTH)

        @pl.when(k > 0)
        def _():
            w_sum(og_at(k - 1))

        return carry

    half_stream = ROWS // 2
    mix_a, mix_b = (
        RingReduce(
            lambda p, r, first=n * half_stream: mixp.at[
                og_place(p, r), :, pl.ds(first, half_stream)
            ],
            m_via.at[n], m_ring.at[n], m_cross.at[n], m_send.at[n], m_rsem.at[n],
            z_plus, z_minus, x_far,
        )
        for n in (0, 1)
    )
    weight = RingReduce(
        lambda p, r: w_pair.at[((y + r) % 4) * 2 + (x + p) % 2], w_via, w_ring, None,
        w_send, w_rsem, y_plus, y_minus, x_near,
    )
    lax.fori_loop(0, 5, projection_step, 0)
    lax.fori_loop(0, 4, functools.partial(mix_step, 1 - xh), 0)
    mix_a.start("far", 1)
    mix_a.start("near", 1)
    mix_b.start("far", 1)
    lax.fori_loop(5, 7, projection_step, 0)
    lax.fori_loop(0, 4, functools.partial(mix_step, xh), 0)
    lax.fori_loop(7, 8, projection_step, 0)
    w_sum(og_at(7))

    turns = [(1, 2), (0, 2), (1, 1), (1, 3), (1, 0), (0, 1), (0, 3), (0, 0)]
    term = RingReduce(
        lambda p, r: t_recv.at[turns.index((p, r))], t_via, t_ring, t_cross,
        t_send, t_rsem, y_plus, y_minus, x_near,
    )

    for h in range(HEADS_DEV):
        grad = head_t[cols_of(h)]
        rounded = grad.astype(BF16)
        head[:, cols_of(h)] = grad.T.astype(BF16)
        stat[1, h : h + 1] = jnp.sum(
            rounded.astype(F32) * att_t[cols_of(h)].astype(F32), axis=0, keepdims=True
        )
        att_t[cols_of(h)] = rounded
        dq[cols_of(h)] = jnp.zeros((HEAD_SIZE, BOTH), F32)
    head_tb = att_t

    def backward_tile(key, value, h, first, masks):
        scores = scores_of(key, h, first) + masks
        probs = jnp.exp2(scores - stat[0, h : h + 1, first:])
        value_term = dot(probs.astype(BF16), head[first:, cols_of(h)])
        prob_grad = dot(value, head_tb[cols_of(h), first:])
        score_grad = (probs * (prob_grad - stat[1, h : h + 1, first:])).astype(BF16)
        key_term = dot(score_grad, q_ref[first:, cols_of(h)]) * SCALE
        dq[cols_of(h), first:] += dot_tn(key, score_grad)
        return key_term.astype(BF16), value_term.astype(BF16)

    def t_copy(j):
        return remote(t_out.at[j], t_recv.at[j], ts_send.at[j], ts_recv.at[j], sibling)

    w_mine = pl.multiple_of(c * half_rows, 16)

    def final_copy():
        part = w_final.at[pl.ds(w_mine, half_rows)]
        return remote(part, part, wf_sem.at[0], wf_sem.at[1], sibling)

    def backward_step(i, carry):
        odd, last, second = i % 2, equal(i, 15), equal(i, 1)
        late = (i + 13) // 16
        d = 1 - ((1 - odd) * late + last + second)
        j = late * (odd * ((i + 1) // 2) + (1 - odd) * (i // 2 - 1) - last) + equal(i, 2)
        p = sum(turn[0] * equal(j, n) for n, turn in enumerate(turns))
        off = sum(turn[1] * equal(j, n) for n, turn in enumerate(turns))
        place = slot((y + off) % 4, (x + p) % 2, (c + d) % 2)

        @pl.when(i == 1)
        def _():
            mix_a.join(1)
            mix_b.start("near", 1)

        @pl.when(i == 6)
        def _():
            mix_b.join(1)
            for part in (mix_a, mix_b):
                part.start("far", 0)
            for part in (mix_a, mix_b):
                part.start("near", 0)

        @pl.when(i == 8)
        def _():
            mix_a.to_partner()

        @pl.when(i == 9)
        def _():
            for n in range(4):
                w_across(n).wait_recv()
                mine = w_pair.at[2 * n + x]
                mine[...] = (mine[...].astype(F32) + w_x[n].astype(F32)).astype(BF16)
            weight.start("far", 0)
            weight.start("near", 0)

        @pl.when(i == 12)
        def _():
            mix_b.to_partner()

        @pl.when(i == 15)
        def _():
            weight.join(0)
            term.join(0)
            term.to_partner()

        set_bias(place)
        for h in range(HEADS_DEV):
            key_term, value_term = backward_tile(
                kv[place, 0, :ROWS, cols_of(h)], kv[place, 1, :ROWS, cols_of(h)], h, 0, bias[...]
            )
            t_mine[0, :, cols_of(h)] = key_term
            t_mine[1, :, cols_of(h)] = value_term

        @pl.when(d == 1)
        def _():
            t_out[j] = t_mine[...]
            t_copy(j).start()

        @pl.when(d == 0)
        def _():
            t_copy(j).wait_recv()
            t_recv[j] = (t_recv[j].astype(F32) + t_mine[...].astype(F32)).astype(BF16)

        for n, (p_now, r) in enumerate(turns):
            if r == 0:
                continue

            @pl.when(i == (2 * n + 2 if n else 1))
            def _():
                if r == 2:
                    term.start("far", p_now)
                else:
                    which = (0,) if r == 1 else (1,)
                    term.start("near", p_now, which)
                    if p_now == 1:
                        term.join(p_now, which)

        return carry

    lax.fori_loop(0, 16, backward_step, 0)

    mix_a.join(0)
    mix_b.join(0)
    bias[:, :ROWS] = self_bias
    for h in range(HEADS_DEV):
        key_term, value_term = backward_tile(
            noisy_kv[0, :, cols_of(h)], noisy_kv[1, :, cols_of(h)], h, ROWS, bias[:, :ROWS]
        )
        kg_ref[1, :, cols_of(h)] = key_term
        vg_ref[1, :, cols_of(h)] = value_term

    for h in range(HEADS_DEV):
        qg_ref[:, cols_of(h)] = (dq[cols_of(h)] * SCALE).T.astype(BF16)


    w_final[pl.ds(w_mine, half_rows)] = weight.gathered(0).reshape(half_rows, WIDTH)
    final_copy().start()
    w_theirs = pl.multiple_of((1 - c) * half_rows, 16)
    part = w_final.at[pl.ds(w_theirs, half_rows)]
    remote(part, part, wf_sem.at[0], wf_sem.at[1], sibling).wait_recv()
    for n in range(INNER_DEV // HEAD_SIZE):
        w_turn[:, cols_of(n)] = w_final[cols_of(n)].T
    wg_ref[...] = w_turn[pl.ds(pl.multiple_of(c * (WIDTH // 2), 8), WIDTH // 2)]

    terms = term.result().astype(BF16)
    kg_ref[0] = terms[0]
    vg_ref[0] = terms[1]
    mixed_ref[:, :half_stream] = mix_a.result().astype(BF16)
    mixed_ref[:, half_stream:] = mix_b.result().astype(BF16)

    for half in (0, 1):
        for kind in ("x", "plus", "minus"):
            own_copy(kind, half).wait_send()
        for kind in ("plus", "minus"):
            near_copy(kind, half).wait_send()
            og_own(kind, half).wait_send()
            og_far(kind, half).wait_send()
        for off in range(4):
            og_late(off, half).wait_send()
        og_own("far", half).wait_send()
        for n in range(8):
            kv_copy(s, half, 2 * n + half, sibling).wait_send()
    for n in range(8):
        w_copy(n).wait_send()
        t_copy(n).wait_send()
    for n in range(4):
        w_across(n).wait_send()
    for p in (0, 1):
        pass_plus(p).wait_send()
        pass_minus(p).wait_send()
        og_pass_plus(p).wait_send()
        og_pass_minus(p).wait_send()
    mix_a.finish()
    mix_b.finish()
    weight.finish((0,))
    term.finish()
    final_copy().wait_send()


def results_kernel(*refs):
    count = len(refs) // 2
    copies = [
        pltpu.make_async_copy(refs[n], refs[count + n], refs[-1].at[n]) for n in range(count)
    ]
    for copy in copies:
        copy.start()
    for copy in copies:
        copy.wait()


def local(queries, keys, values, block_order, out_weight, out_grad):
    unit = (2, ROWS, INNER_DEV)
    w_unit = (2, INNER_DEV // 4, WIDTH)
    m_unit = (2, ROWS, WIDTH)

    def buffer(*shape, dtype=BF16):
        return pltpu.VMEM(shape, dtype)

    def sums(u, *parts):
        return [buffer(*parts, 2, *u), buffer(*parts, 2, 2, *u), buffer(*parts, *u)]

    scratch = [
        buffer(16, 2, ROWS + POS_ROWS, INNER_DEV),
        buffer(*unit),
        buffer(*out_weight.shape),
        buffer(BOTH, INNER_DEV),
        buffer(8, *m_unit),
        buffer(8, BOTH, dtype=F32),
        buffer(HEADS_DEV, 2 * HEAD_SIZE, BOTH),
        buffer(INNER_DEV, BOTH, dtype=F32),
        buffer(2, 8, BOTH, dtype=F32),
        buffer(INNER_DEV, BOTH),
        buffer(BOTH, INNER_DEV),
        buffer(ROWS, BOTH, dtype=F32),
        buffer(INNER_DEV, BOTH, dtype=F32),
        buffer(BOTH, INNER_DEV),
        buffer(INNER_DEV, BOTH, dtype=F32),
        buffer(8, *m_unit), *sums((2, ROWS // 2, WIDTH), 2),
        buffer(8, *w_unit), buffer(8, *w_unit), buffer(8, *w_unit), buffer(4, *w_unit),
        *sums(w_unit)[:2], buffer(INNER_DEV, WIDTH, dtype=F32),
        buffer(WIDTH, INNER_DEV, dtype=F32),
        buffer(8, *unit), buffer(8, *unit), buffer(*unit), *sums(unit),
        *(
            pltpu.SemaphoreType.DMA(shape)
            for shape in (
                (7,), (30,), (16, 2), (22,), (8, 4), (2, 13), (2, 13), (13,), (13,),
                (8,), (8,), (4,), (4,), (2,), (13,), (13,), (8,), (8,),
            )
        ),
    ]
    whole = pl.BlockSpec(memory_space=pltpu.VMEM)
    anywhere = pl.BlockSpec(memory_space=pl.ANY)
    shapes = (
        jax.ShapeDtypeStruct(m_unit, BF16),
        jax.ShapeDtypeStruct((BOTH, INNER_DEV), BF16),
        jax.ShapeDtypeStruct(unit, BF16),
        jax.ShapeDtypeStruct(unit, BF16),
        jax.ShapeDtypeStruct((WIDTH // 2, INNER_DEV), F32),
    )
    results = pl.pallas_call(
        layer_kernel,
        out_shape=shapes,
        in_specs=[pl.BlockSpec(memory_space=pltpu.SMEM)] + [anywhere] * 5,
        out_specs=(whole,) * 5,
        scratch_shapes=scratch,
        compiler_params=pltpu.CompilerParams(
            collective_id=0, has_side_effects=True, vmem_limit_bytes=63 * 2**20
        ),
    )(block_order, queries.reshape(BOTH, INNER_DEV), keys, values, out_weight, out_grad)
    mixed, query_grad, key_grad, value_grad, weight_grad = pl.pallas_call(
        results_kernel,
        out_shape=shapes,
        in_specs=[whole] * 5,
        out_specs=(anywhere,) * 5,
        scratch_shapes=[pltpu.SemaphoreType.DMA((5,))],
    )(*results)
    return (mixed, query_grad.reshape(unit), key_grad, value_grad, weight_grad.T)


def solution(mesh):
    return jax.shard_map(
        local,
        mesh=mesh,
        in_specs=(
            P(None, "seq", "tp"),
            P(None, "seq", "tp"),
            P(None, "seq", "tp"),
            P("seq"),
            P("tp", None),
            P(None, "seq", "tp"),
        ),
        out_specs=(
            P(None, "seq", "tp"),
            P(None, "seq", "tp"),
            P(None, "seq", "tp"),
            P(None, "seq", "tp"),
            P("tp", "seq"),
        ),
        check_vma=False,
    )
```

```python
import functools
import math

import jax
import jax.numpy as jnp
from jax import lax
from jax.experimental import pallas as pl
from jax.experimental.pallas import tpu as pltpu
from jax.sharding import PartitionSpec as P

HEAD_SIZE = 128
BLOCK = 16
HEADS_DEV = 3
ROWS = 256
BOTH = 2 * ROWS
POS_ROWS = ROWS // BLOCK
INNER_DEV = HEADS_DEV * HEAD_SIZE
SPLIT = 192
WIDTH = 640
MESH = pl.DeviceIdType.MESH
F32 = jnp.float32
BF16 = jnp.bfloat16
MASKED = -1e30
LOWEST = -1e29
LOG2_SCALE = math.log2(math.e) / math.sqrt(HEAD_SIZE)
SCALE = 1.0 / math.sqrt(HEAD_SIZE)


def dot(a, b):
    return lax.dot_general(a, b, (((1,), (0,)), ((), ())), preferred_element_type=F32)


def dot_nt(a, b):
    return lax.dot_general(a, b, (((1,), (1,)), ((), ())), preferred_element_type=F32)


def dot_tn(a, b):
    return lax.dot_general(a, b, (((0,), (0,)), ((), ())), preferred_element_type=F32)


def remote(src, dst, send_sem, recv_sem, device):
    return pltpu.make_async_remote_copy(
        src_ref=src,
        dst_ref=dst,
        send_sem=send_sem,
        recv_sem=recv_sem,
        device_id=device,
        device_id_type=MESH,
    )


def equal(a, n):
    return (a + 16 - n) // 16 - (a + 15 - n) // 16


class RingReduce:
    def __init__(self, piece, via, ring, cross, send, recv, plus, minus, partner):
        self.piece, self.via, self.ring, self.cross = piece, via, ring, cross
        self.send, self.recv = send, recv
        self.plus, self.minus, self.partner = plus, minus, partner

    def copy(self, kind, p, n):
        if kind == "cross":
            return remote(
                self.piece(1, 0), self.cross, self.send.at[12], self.recv.at[12], self.partner
            )
        at = 6 * p + 2 * ("far", "near", "joint").index(kind) + n
        half = 1 - n if kind == "near" else n
        source = self.piece(p, 2 if kind == "far" else (1, 3)[n]).at[half]
        target = self.via.at[p, n] if kind == "far" else self.ring.at[p, n, half]
        device = (self.plus, self.minus)[n]
        return remote(source, target, self.send.at[at], self.recv.at[at], device)

    def start(self, kind, p, which=(0, 1)):
        for n in which:
            self.copy(kind, p, n).start()

    def join(self, p, which=(0, 1)):
        for n in which:
            self.copy("far", p, n).wait_recv()
            target = self.piece(p, (1, 3)[n])
            target[n] = (target[n].astype(F32) + self.via[p, n].astype(F32)).astype(BF16)
            self.copy("joint", p, n).start()

    def gathered(self, p):
        for kind in ("near", "joint"):
            for n in (0, 1):
                self.copy(kind, p, n).wait_recv()
        own = self.piece(p, 0)
        return own[...].astype(F32) + self.ring[p, 0].astype(F32) + self.ring[p, 1].astype(F32)

    def to_partner(self):
        total = self.gathered(1)
        self.piece(1, 0)[...] = total.astype(BF16)
        self.copy("cross", 1, 0).start()

    def result(self):
        total = self.gathered(0)
        self.copy("cross", 1, 0).wait_recv()
        return total + self.cross[...].astype(F32)

    def finish(self, sides=(0, 1)):
        for p in sides:
            for kind in ("far", "near", "joint"):
                for n in (0, 1):
                    self.copy(kind, p, n).wait_send()
        if 1 in sides:
            self.copy("cross", 1, 0).wait_send()


def layer_kernel(
    order_ref, q_in, k_ref, v_ref, weight_ref, og_ref,
    mixed_ref, qg_ref, kg_ref, vg_ref, wg_ref,
    kv, noisy_kv, w_ref, q_ref, og, limit, qt, acc, stat, att_t, att, bias, head_t, head, dq,
    mixp, m_via, m_ring, m_cross,
    w_pair, w_out, w_recv, w_x, w_via, w_ring, w_final, w_turn,
    t_out, t_recv, t_mine, t_via, t_ring, t_cross,
    load, kv_send, kv_recv, og_send, og_recv,
    m_send, m_rsem, w_send, w_rsem, ws_send, ws_recv, wx_send, wx_recv, wf_sem,
    t_send, t_rsem, ts_send, ts_recv,
):
    s = lax.axis_index("seq")
    t = lax.axis_index("tp")
    y, x, c = s // 4, (s // 2) % 2, s % 2
    xh, z = t // 4, t % 4

    def slot(ys, xs, cs):
        return (ys * 2 + xs) * 2 + cs

    y_plus = {"seq": slot((y + 1) % 4, x, c)}
    y_minus = {"seq": slot((y + 3) % 4, x, c)}
    x_near = {"seq": slot(y, 1 - x, c)}
    sibling = {"seq": slot(y, x, 1 - c)}
    z_plus = {"tp": xh * 4 + (z + 1) % 4}
    z_minus = {"tp": xh * 4 + (z + 3) % 4}
    x_far = {"tp": (1 - xh) * 4 + z}

    barrier = pltpu.get_barrier_semaphore()
    partners = (y_plus, y_minus, x_near, sibling, z_plus, z_minus, x_far)
    for partner in partners:
        pl.semaphore_signal(barrier, inc=1, device_id=partner, device_id_type=MESH)

    loads = [
        pltpu.make_async_copy(src, dst, load.at[n])
        for n, (src, dst) in enumerate(
            (
                (k_ref.at[0], kv.at[s, 0, pl.ds(0, ROWS)]),
                (v_ref.at[0], kv.at[s, 1, pl.ds(0, ROWS)]),
                (og_ref, og.at[t]),
                (k_ref.at[1], noisy_kv.at[0]),
                (v_ref.at[1], noisy_kv.at[1]),
                (weight_ref, w_ref),
                (q_in, q_ref),
            )
        )
    ]
    for copy in loads[:3]:
        copy.start()

    mark_row = lax.broadcasted_iota(jnp.int32, (POS_ROWS, INNER_DEV), 0)
    lane = lax.broadcasted_iota(jnp.int32, (8, BOTH), 1)
    lane_block = (lane % ROWS) // BLOCK
    marks = jnp.zeros((POS_ROWS, INNER_DEV), F32)
    start = jnp.zeros((8, BOTH), F32)
    for b in range(POS_ROWS):
        position = order_ref[b].astype(F32)
        marks = jnp.where(mark_row == b, position, marks)
        start = jnp.where(lane_block == b, position * float(BLOCK), start)
    kv[s, 0, ROWS:] = marks.astype(BF16)
    limit[...] = start + jnp.where(lane < ROWS, lane % BLOCK, -1).astype(F32)

    def kv_copy(place, half, sem, device):
        part = kv.at[place, half, pl.ds(0, ROWS if half else ROWS + POS_ROWS)]
        return remote(part, part, kv_send.at[sem], kv_recv.at[place, half], device)

    near_place = slot(y, 1 - x, c)

    def ring_place(p, off):
        return slot((y + off) % 4, (x + p) % 2, c)

    def own_copy(kind, half):
        at = {"sibling": 0, "x": 16, "plus": 18, "minus": 20}[kind] + half
        device = {"sibling": sibling, "x": x_near, "plus": y_plus, "minus": y_minus}[kind]
        return kv_copy(s, half, at, device)

    def near_copy(kind, half):
        at = {"plus": 22, "minus": 24}[kind] + half
        return kv_copy(near_place, half, at, {"plus": y_plus, "minus": y_minus}[kind])

    def pass_plus(p):
        return kv_copy(ring_place(p, 3), 0, 26 + 2 * p, y_plus)

    def pass_minus(p):
        return kv_copy(ring_place(p, 1), 1, 27 + 2 * p, y_minus)

    def og_copy(place, half, sem, device, part=None):
        rows = {None: pl.ds(0, ROWS), 0: pl.ds(0, SPLIT), 1: pl.ds(SPLIT, ROWS - SPLIT)}[part]
        piece = og.at[place, half, rows]
        recv = og_recv.at[place, half + (2 if part == 1 else 0)]
        return remote(piece, piece, og_send.at[sem], recv, device)

    far_place = (1 - xh) * 4 + z

    def og_own(kind, half):
        if kind == "far":
            return og_copy(t, half, half, x_far, 0)
        at = {"plus": 2, "minus": 4}[kind] + half
        return og_copy(t, half, at, {"plus": z_plus, "minus": z_minus}[kind])

    def og_far(kind, half):
        at = {"plus": 6, "minus": 8}[kind] + half
        return og_copy(far_place, half, at, {"plus": z_plus, "minus": z_minus}[kind], 0)

    def og_place(a, off):
        return ((xh + a) % 2) * 4 + (z + off) % 4

    def og_pass_plus(a):
        return og_copy(og_place(a, 3), 0, 10 + 2 * a, z_plus, 0 if a else None)

    def og_pass_minus(a):
        return og_copy(og_place(a, 1), 1, 11 + 2 * a, z_minus, 0 if a else None)

    def og_late(off, half):
        return og_copy(og_place(0, off), half, 14 + 2 * off + half, x_far, 1)

    def og_wait(place, halves=(0, 1), part=None):
        for half in halves:
            og_copy(place, half, 0, z_plus, part).wait_recv()

    loads[0].wait()
    loads[1].wait()
    loads[2].wait()
    pl.semaphore_wait(barrier, len(partners))
    for n in (0, 1):
        own_copy("x", n).start()
        own_copy("plus", n).start()
        own_copy("minus", 1 - n).start()
    for n in (0, 1):
        og_own("plus", n).start()
        og_own("minus", 1 - n).start()
        og_own("far", n).start()
        own_copy("sibling", n).start()
    for n in (0, 1):
        og_late(0, n).start()
    for n in (6, 3, 4, 5):
        loads[n].start()
    loads[6].wait()

    for h in range(HEADS_DEV):
        cols = slice(h * HEAD_SIZE, (h + 1) * HEAD_SIZE)
        scaled = q_ref[:, cols].astype(F32).T * LOG2_SCALE
        high = scaled.astype(BF16)
        qt[h, :HEAD_SIZE] = high
        qt[h, HEAD_SIZE:] = (scaled - high.astype(F32)).astype(BF16)

    def cols_of(h):
        return slice(h * HEAD_SIZE, (h + 1) * HEAD_SIZE)

    def scores_of(key, h, first):
        return dot(jnp.concatenate([key, key], axis=1), qt[h, :, first:])

    loads[3].wait()
    loads[4].wait()
    row_block = lax.broadcasted_iota(jnp.int32, (ROWS, ROWS), 0) // BLOCK
    col_block = lax.broadcasted_iota(jnp.int32, (ROWS, ROWS), 1) // BLOCK
    self_bias = jnp.where(row_block == col_block, 0.0, MASKED).astype(F32)
    bias[:, :ROWS] = self_bias

    for h in range(HEADS_DEV):
        scores = scores_of(noisy_kv[0, :, cols_of(h)], h, ROWS) + bias[:, :ROWS]
        top = jnp.max(scores, axis=0, keepdims=True)
        weights = jnp.exp2(scores - top)
        stat[0, h : h + 1, :ROWS] = jnp.full((1, ROWS), LOWEST, F32)
        stat[0, h : h + 1, ROWS:] = top
        stat[1, h : h + 1, :ROWS] = jnp.zeros((1, ROWS), F32)
        stat[1, h : h + 1, ROWS:] = jnp.sum(weights, axis=0, keepdims=True)
        acc[cols_of(h), :ROWS] = jnp.zeros((HEAD_SIZE, ROWS), F32)
        acc[cols_of(h), ROWS:] = dot_tn(noisy_kv[1, :, cols_of(h)], weights.astype(BF16))

    def set_bias(place):
        position = kv[place, 0, ROWS:, :HEAD_SIZE].astype(F32)
        offset = lax.broadcasted_iota(jnp.int32, (BLOCK, HEAD_SIZE), 0).astype(F32)
        for b in range(POS_ROWS):
            code = position[b : b + 1] * float(BLOCK) + offset
            for n in range(BOTH // HEAD_SIZE):
                lanes = slice(n * HEAD_SIZE, (n + 1) * HEAD_SIZE)
                bias[b * BLOCK : (b + 1) * BLOCK, lanes] = jnp.where(
                    code <= limit[0:1, lanes], 0.0, MASKED
                ).astype(F32)

    def columns(j):
        return pl.ds(pl.multiple_of(j * WIDTH, HEAD_SIZE), WIDTH)

    half_rows = INNER_DEV // 2
    head_t[...] = jnp.zeros((INNER_DEV, BOTH), F32)

    loads[5].wait()

    og_order = ((0, 0), (0, 3), (0, 1), (1, 0), (0, 2), (1, 3), (1, 1), (1, 2))

    def og_at(k):
        a = sum(u[0] * equal(k, n) for n, u in enumerate(og_order))
        off = sum(u[1] * equal(k, n) for n, u in enumerate(og_order))
        return og_place(a, off)

    def head_step(k, carry):
        j = og_at(k)
        head_t[...] += dot_nt(w_ref[:, columns(j)], og[j].reshape(BOTH, WIDTH))
        return carry

    def forward_step(i, carry):
        n, d = i // 2, i % 2
        p = n // 5 + (n + 6) // 7 - (n + 5) // 7
        m = (n + 1) % 3
        off = ((n + 6) // 8) * (m + 3 * ((2 - m) // 2))
        place = slot((y + off) % 4, (x + p) % 2, (c + d) % 2)

        @pl.when(i == 6)
        def _():
            og_wait(og_place(0, 3), (0,))
            og_pass_plus(0).start()
            og_wait(og_place(0, 1), (1,))
            og_pass_minus(0).start()

        @pl.when(i == 8)
        def _():
            og_wait(far_place, (0,), 0)
            og_far("plus", 0).start()
            og_wait(og_place(0, 3), (1,))
            og_wait(og_place(0, 1), (0,))
            for off in (3, 1):
                for half in (0, 1):
                    og_late(off, half).start()

        @pl.when(i == 12)
        def _():
            og_wait(og_place(0, 2))
            for half in (0, 1):
                og_late(2, half).start()

        @pl.when(i == 10)
        def _():
            og_wait(far_place, (1,), 0)
            og_far("minus", 1).start()
            og_far("plus", 1).start()
            og_far("minus", 0).start()

        @pl.when(i == 14)
        def _():
            og_wait(far_place, (0, 1), 1)
            lax.fori_loop(0, 5, head_step, 0)

        for half in (0, 1):

            @pl.when(i > 0)
            def _():
                kv_copy(place, half, 0, sibling).wait_recv()

            @pl.when(i == 2)
            def _():
                near_copy("plus", half).start()
                near_copy("minus", half).start()

            for side, at in ((0, 4), (1, 10)):

                @pl.when(i == at + 2 * half)
                def _():
                    (pass_minus if half else pass_plus)(side).start()

            @pl.when((i > 0) & (d == 0))
            def _():
                kv_copy(place, half, 2 * n + half, sibling).start()

        set_bias(place)
        for h in range(HEADS_DEV):
            scores = scores_of(kv[place, 0, :ROWS, cols_of(h)], h, 0) + bias[...]
            old = stat[0, h : h + 1]
            top = jnp.maximum(old, jnp.max(scores, axis=0, keepdims=True))
            weights = jnp.exp2(scores - top)
            factor = jnp.exp2(old - top)
            stat[0, h : h + 1] = top
            stat[1, h : h + 1] = stat[1, h : h + 1] * factor + jnp.sum(
                weights, axis=0, keepdims=True
            )
            acc[cols_of(h)] = acc[cols_of(h)] * factor + dot_tn(
                kv[place, 1, :ROWS, cols_of(h)], weights.astype(BF16)
            )
        return carry

    lax.fori_loop(0, 16, forward_step, 0)
    og_wait(og_place(1, 3), (0,), 0)
    og_pass_plus(1).start()
    og_wait(og_place(1, 1), (1,), 0)
    og_pass_minus(1).start()

    for h in range(HEADS_DEV):
        total = stat[1, h : h + 1]
        out = acc[cols_of(h)] / total
        att_t[cols_of(h)] = out.astype(BF16)
        att[:, cols_of(h)] = out.T.astype(BF16)
        stat[0, h : h + 1] = stat[0, h : h + 1] + jnp.log2(total)

    def mix_step(side, n, carry):
        j = side * 4 + n
        mixp[j] = dot(att[...], w_ref[:, columns(j)]).astype(BF16).reshape(2, ROWS, WIDTH)
        return carry

    def w_copy(j):
        return remote(w_out.at[j], w_recv.at[j], ws_send.at[j], ws_recv.at[j], sibling)

    def w_across(n):
        return remote(w_pair.at[2 * n + 1 - x], w_x.at[n], wx_send.at[n], wx_recv.at[n], x_near)

    def w_sum(j):
        w_copy(j).wait_recv()
        w_pair[j] = (w_pair[j].astype(F32) + w_recv[j].astype(F32)).astype(BF16)

        @pl.when(j % 2 == 1 - x)
        def _():
            w_across(j // 2).start()

    def projection_step(k, carry):
        j = og_at(k)

        for half, pieces in enumerate(((6, 7), (5, 7))):
            for n in pieces:

                @pl.when(k == n)
                def _():
                    og_wait(j, (half,), 0)

        @pl.when(k > 4)
        def _():
            og_wait(j, (0, 1), 1)
            head_step(k, 0)

        grads = og[j].reshape(BOTH, WIDTH)
        theirs = att_t[pl.ds(pl.multiple_of((1 - c) * half_rows, 16), half_rows)]
        w_out[j] = dot(theirs, grads).astype(BF16).reshape(2, half_rows // 2, WIDTH)
        w_copy(j).start()
        mine = att_t[pl.ds(pl.multiple_of(c * half_rows, 16), half_rows)]
        w_pair[j] = dot(mine, grads).astype(BF16).reshape(2, half_rows // 2, WIDTH)

        @pl.when(k > 0)
        def _():
            w_sum(og_at(k - 1))

        return carry

    half_stream = ROWS // 2
    mix_a, mix_b = (
        RingReduce(
            lambda p, r, first=n * half_stream: mixp.at[
                og_place(p, r), :, pl.ds(first, half_stream)
            ],
            m_via.at[n], m_ring.at[n], m_cross.at[n], m_send.at[n], m_rsem.at[n],
            z_plus, z_minus, x_far,
        )
        for n in (0, 1)
    )
    weight = RingReduce(
        lambda p, r: w_pair.at[((y + r) % 4) * 2 + (x + p) % 2], w_via, w_ring, None,
        w_send, w_rsem, y_plus, y_minus, x_near,
    )
    lax.fori_loop(0, 5, projection_step, 0)
    lax.fori_loop(0, 4, functools.partial(mix_step, 1 - xh), 0)
    mix_a.start("far", 1)
    mix_a.start("near", 1)
    mix_b.start("far", 1)
    lax.fori_loop(5, 7, projection_step, 0)
    lax.fori_loop(0, 4, functools.partial(mix_step, xh), 0)
    lax.fori_loop(7, 8, projection_step, 0)
    w_sum(og_at(7))

    turns = [(1, 2), (0, 2), (1, 1), (1, 3), (1, 0), (0, 1), (0, 3), (0, 0)]
    term = RingReduce(
        lambda p, r: t_recv.at[turns.index((p, r))], t_via, t_ring, t_cross,
        t_send, t_rsem, y_plus, y_minus, x_near,
    )

    for h in range(HEADS_DEV):
        grad = head_t[cols_of(h)]
        rounded = grad.astype(BF16)
        head[:, cols_of(h)] = grad.T.astype(BF16)
        stat[1, h : h + 1] = jnp.sum(
            rounded.astype(F32) * att_t[cols_of(h)].astype(F32), axis=0, keepdims=True
        )
        att_t[cols_of(h)] = rounded
        dq[cols_of(h)] = jnp.zeros((HEAD_SIZE, BOTH), F32)
    head_tb = att_t

    def backward_tile(key, value, h, first, masks):
        scores = scores_of(key, h, first) + masks
        probs = jnp.exp2(scores - stat[0, h : h + 1, first:])
        value_term = dot(probs.astype(BF16), head[first:, cols_of(h)])
        prob_grad = dot(value, head_tb[cols_of(h), first:])
        score_grad = (probs * (prob_grad - stat[1, h : h + 1, first:])).astype(BF16)
        key_term = dot(score_grad, q_ref[first:, cols_of(h)]) * SCALE
        dq[cols_of(h), first:] += dot_tn(key, score_grad)
        return key_term.astype(BF16), value_term.astype(BF16)

    def t_copy(j):
        return remote(t_out.at[j], t_recv.at[j], ts_send.at[j], ts_recv.at[j], sibling)

    w_mine = pl.multiple_of(c * half_rows, 16)

    def final_copy():
        part = w_final.at[pl.ds(w_mine, half_rows)]
        return remote(part, part, wf_sem.at[0], wf_sem.at[1], sibling)

    def backward_step(i, carry):
        odd, last, second = i % 2, equal(i, 15), equal(i, 1)
        late = (i + 13) // 16
        d = 1 - ((1 - odd) * late + last + second)
        j = late * (odd * ((i + 1) // 2) + (1 - odd) * (i // 2 - 1) - last) + equal(i, 2)
        p = sum(turn[0] * equal(j, n) for n, turn in enumerate(turns))
        off = sum(turn[1] * equal(j, n) for n, turn in enumerate(turns))
        place = slot((y + off) % 4, (x + p) % 2, (c + d) % 2)

        @pl.when(i == 1)
        def _():
            mix_a.join(1)
            mix_b.start("near", 1)

        @pl.when(i == 6)
        def _():
            mix_b.join(1)
            for part in (mix_a, mix_b):
                part.start("far", 0)
            for part in (mix_a, mix_b):
                part.start("near", 0)

        @pl.when(i == 8)
        def _():
            mix_a.to_partner()

        @pl.when(i == 9)
        def _():
            for n in range(4):
                w_across(n).wait_recv()
                mine = w_pair.at[2 * n + x]
                mine[...] = (mine[...].astype(F32) + w_x[n].astype(F32)).astype(BF16)
            weight.start("far", 0)
            weight.start("near", 0)

        @pl.when(i == 12)
        def _():
            mix_b.to_partner()

        @pl.when(i == 15)
        def _():
            weight.join(0)
            term.join(0)
            term.to_partner()

        set_bias(place)
        for h in range(HEADS_DEV):
            key_term, value_term = backward_tile(
                kv[place, 0, :ROWS, cols_of(h)], kv[place, 1, :ROWS, cols_of(h)], h, 0, bias[...]
            )
            t_mine[0, :, cols_of(h)] = key_term
            t_mine[1, :, cols_of(h)] = value_term

        @pl.when(d == 1)
        def _():
            t_out[j] = t_mine[...]
            t_copy(j).start()

        @pl.when(d == 0)
        def _():
            t_copy(j).wait_recv()
            t_recv[j] = (t_recv[j].astype(F32) + t_mine[...].astype(F32)).astype(BF16)

        for n, (p_now, r) in enumerate(turns):
            if r == 0:
                continue

            @pl.when(i == (2 * n + 2 if n else 1))
            def _():
                if r == 2:
                    term.start("far", p_now)
                else:
                    which = (0,) if r == 1 else (1,)
                    term.start("near", p_now, which)
                    if p_now == 1:
                        term.join(p_now, which)

        return carry

    lax.fori_loop(0, 16, backward_step, 0)

    mix_a.join(0)
    mix_b.join(0)
    bias[:, :ROWS] = self_bias
    for h in range(HEADS_DEV):
        key_term, value_term = backward_tile(
            noisy_kv[0, :, cols_of(h)], noisy_kv[1, :, cols_of(h)], h, ROWS, bias[:, :ROWS]
        )
        kg_ref[1, :, cols_of(h)] = key_term
        vg_ref[1, :, cols_of(h)] = value_term

    for h in range(HEADS_DEV):
        qg_ref[:, cols_of(h)] = (dq[cols_of(h)] * SCALE).T.astype(BF16)


    w_final[pl.ds(w_mine, half_rows)] = weight.gathered(0).reshape(half_rows, WIDTH)
    final_copy().start()
    w_theirs = pl.multiple_of((1 - c) * half_rows, 16)
    part = w_final.at[pl.ds(w_theirs, half_rows)]
    remote(part, part, wf_sem.at[0], wf_sem.at[1], sibling).wait_recv()
    for n in range(INNER_DEV // HEAD_SIZE):
        w_turn[:, cols_of(n)] = w_final[cols_of(n)].T
    wg_ref[...] = w_turn[pl.ds(pl.multiple_of(c * (WIDTH // 2), 8), WIDTH // 2)]

    terms = term.result().astype(BF16)
    kg_ref[0] = terms[0]
    vg_ref[0] = terms[1]
    mixed_ref[:, :half_stream] = mix_a.result().astype(BF16)
    mixed_ref[:, half_stream:] = mix_b.result().astype(BF16)

    for half in (0, 1):
        for kind in ("x", "plus", "minus"):
            own_copy(kind, half).wait_send()
        for kind in ("plus", "minus"):
            near_copy(kind, half).wait_send()
            og_own(kind, half).wait_send()
            og_far(kind, half).wait_send()
        for off in range(4):
            og_late(off, half).wait_send()
        og_own("far", half).wait_send()
        for n in range(8):
            kv_copy(s, half, 2 * n + half, sibling).wait_send()
    for n in range(8):
        w_copy(n).wait_send()
        t_copy(n).wait_send()
    for n in range(4):
        w_across(n).wait_send()
    for p in (0, 1):
        pass_plus(p).wait_send()
        pass_minus(p).wait_send()
        og_pass_plus(p).wait_send()
        og_pass_minus(p).wait_send()
    mix_a.finish()
    mix_b.finish()
    weight.finish((0,))
    term.finish()
    final_copy().wait_send()


def results_kernel(*refs):
    count = len(refs) // 2
    copies = [
        pltpu.make_async_copy(refs[n], refs[count + n], refs[-1].at[n]) for n in range(count)
    ]
    for copy in copies:
        copy.start()
    for copy in copies:
        copy.wait()


def local(queries, keys, values, block_order, out_weight, out_grad):
    unit = (2, ROWS, INNER_DEV)
    w_unit = (2, INNER_DEV // 4, WIDTH)
    m_unit = (2, ROWS, WIDTH)

    def buffer(*shape, dtype=BF16):
        return pltpu.VMEM(shape, dtype)

    def sums(u, *parts):
        return [buffer(*parts, 2, *u), buffer(*parts, 2, 2, *u), buffer(*parts, *u)]

    scratch = [
        buffer(16, 2, ROWS + POS_ROWS, INNER_DEV),
        buffer(*unit),
        buffer(*out_weight.shape),
        buffer(BOTH, INNER_DEV),
        buffer(8, *m_unit),
        buffer(8, BOTH, dtype=F32),
        buffer(HEADS_DEV, 2 * HEAD_SIZE, BOTH),
        buffer(INNER_DEV, BOTH, dtype=F32),
        buffer(2, 8, BOTH, dtype=F32),
        buffer(INNER_DEV, BOTH),
        buffer(BOTH, INNER_DEV),
        buffer(ROWS, BOTH, dtype=F32),
        buffer(INNER_DEV, BOTH, dtype=F32),
        buffer(BOTH, INNER_DEV),
        buffer(INNER_DEV, BOTH, dtype=F32),
        buffer(8, *m_unit), *sums((2, ROWS // 2, WIDTH), 2),
        buffer(8, *w_unit), buffer(8, *w_unit), buffer(8, *w_unit), buffer(4, *w_unit),
        *sums(w_unit)[:2], buffer(INNER_DEV, WIDTH, dtype=F32),
        buffer(WIDTH, INNER_DEV, dtype=F32),
        buffer(8, *unit), buffer(8, *unit), buffer(*unit), *sums(unit),
        *(
            pltpu.SemaphoreType.DMA(shape)
            for shape in (
                (7,), (30,), (16, 2), (22,), (8, 4), (2, 13), (2, 13), (13,), (13,),
                (8,), (8,), (4,), (4,), (2,), (13,), (13,), (8,), (8,),
            )
        ),
    ]
    whole = pl.BlockSpec(memory_space=pltpu.VMEM)
    anywhere = pl.BlockSpec(memory_space=pl.ANY)
    shapes = (
        jax.ShapeDtypeStruct(m_unit, BF16),
        jax.ShapeDtypeStruct((BOTH, INNER_DEV), BF16),
        jax.ShapeDtypeStruct(unit, BF16),
        jax.ShapeDtypeStruct(unit, BF16),
        jax.ShapeDtypeStruct((WIDTH // 2, INNER_DEV), F32),
    )
    results = pl.pallas_call(
        layer_kernel,
        out_shape=tuple(pltpu.VMEM(a.shape, a.dtype) for a in shapes),
        in_specs=[pl.BlockSpec(memory_space=pltpu.SMEM)] + [anywhere] * 5,
        out_specs=(whole,) * 5,
        scratch_shapes=scratch,
        compiler_params=pltpu.CompilerParams(
            collective_id=0, has_side_effects=True, vmem_limit_bytes=60 * 2**20
        ),
    )(block_order, queries.reshape(BOTH, INNER_DEV), keys, values, out_weight, out_grad)
    mixed, query_grad, key_grad, value_grad, weight_grad = pl.pallas_call(
        results_kernel,
        out_shape=shapes,
        in_specs=[whole] * 5,
        out_specs=(anywhere,) * 5,
        scratch_shapes=[pltpu.SemaphoreType.DMA((5,))],
    )(*(pltpu.with_memory_space_constraint(a, pltpu.VMEM) for a in results))
    return (mixed, query_grad.reshape(unit), key_grad, value_grad, weight_grad.T)


def solution(mesh):
    return jax.shard_map(
        local,
        mesh=mesh,
        in_specs=(
            P(None, "seq", "tp"),
            P(None, "seq", "tp"),
            P(None, "seq", "tp"),
            P("seq"),
            P("tp", None),
            P(None, "seq", "tp"),
        ),
        out_specs=(
            P(None, "seq", "tp"),
            P(None, "seq", "tp"),
            P(None, "seq", "tp"),
            P(None, "seq", "tp"),
            P("tp", "seq"),
        ),
        check_vma=False,
    )
```

```python
import functools
import math

import jax
import jax.numpy as jnp
from jax import lax
from jax.experimental import pallas as pl
from jax.experimental.pallas import tpu as pltpu
from jax.sharding import PartitionSpec as P

HEAD_SIZE = 128
BLOCK = 16
HEADS_DEV = 3
ROWS = 256
BOTH = 2 * ROWS
POS_ROWS = ROWS // BLOCK
INNER_DEV = HEADS_DEV * HEAD_SIZE
SPLIT = 192
WIDTH = 640
MESH = pl.DeviceIdType.MESH
F32 = jnp.float32
BF16 = jnp.bfloat16
MASKED = -1e30
LOWEST = -1e29
LOG2_SCALE = math.log2(math.e) / math.sqrt(HEAD_SIZE)
SCALE = 1.0 / math.sqrt(HEAD_SIZE)


def dot(a, b):
    return lax.dot_general(a, b, (((1,), (0,)), ((), ())), preferred_element_type=F32)


def dot_nt(a, b):
    return lax.dot_general(a, b, (((1,), (1,)), ((), ())), preferred_element_type=F32)


def dot_tn(a, b):
    return lax.dot_general(a, b, (((0,), (0,)), ((), ())), preferred_element_type=F32)


def remote(src, dst, send_sem, recv_sem, device):
    return pltpu.make_async_remote_copy(
        src_ref=src,
        dst_ref=dst,
        send_sem=send_sem,
        recv_sem=recv_sem,
        device_id=device,
        device_id_type=MESH,
    )


def equal(a, n):
    return (a + 16 - n) // 16 - (a + 15 - n) // 16


class RingReduce:
    def __init__(self, piece, via, ring, cross, send, recv, plus, minus, partner):
        self.piece, self.via, self.ring, self.cross = piece, via, ring, cross
        self.send, self.recv = send, recv
        self.plus, self.minus, self.partner = plus, minus, partner

    def copy(self, kind, p, n):
        if kind == "cross":
            return remote(
                self.piece(1, 0), self.cross, self.send.at[12], self.recv.at[12], self.partner
            )
        at = 6 * p + 2 * ("far", "near", "joint").index(kind) + n
        half = 1 - n if kind == "near" else n
        source = self.piece(p, 2 if kind == "far" else (1, 3)[n]).at[half]
        target = self.via.at[p, n] if kind == "far" else self.ring.at[p, n, half]
        device = (self.plus, self.minus)[n]
        return remote(source, target, self.send.at[at], self.recv.at[at], device)

    def start(self, kind, p, which=(0, 1)):
        for n in which:
            self.copy(kind, p, n).start()

    def join(self, p, which=(0, 1)):
        for n in which:
            self.copy("far", p, n).wait_recv()
            target = self.piece(p, (1, 3)[n])
            target[n] = (target[n].astype(F32) + self.via[p, n].astype(F32)).astype(BF16)
            self.copy("joint", p, n).start()

    def gathered(self, p):
        for kind in ("near", "joint"):
            for n in (0, 1):
                self.copy(kind, p, n).wait_recv()
        own = self.piece(p, 0)
        return own[...].astype(F32) + self.ring[p, 0].astype(F32) + self.ring[p, 1].astype(F32)

    def to_partner(self):
        total = self.gathered(1)
        self.piece(1, 0)[...] = total.astype(BF16)
        self.copy("cross", 1, 0).start()

    def result(self):
        total = self.gathered(0)
        self.copy("cross", 1, 0).wait_recv()
        return total + self.cross[...].astype(F32)

    def finish(self, sides=(0, 1)):
        for p in sides:
            for kind in ("far", "near", "joint"):
                for n in (0, 1):
                    self.copy(kind, p, n).wait_send()
        if 1 in sides:
            self.copy("cross", 1, 0).wait_send()


def layer_kernel(
    order_ref, q_in, k_ref, v_ref, weight_ref, og_ref,
    mixed_ref, qg_ref, kg_ref, vg_ref, wg_ref,
    kv, noisy_kv, w_ref, q_ref, og, limit, qt, acc, stat, att_t, att, bias, head_t, head, dq,
    mixp, m_via, m_ring, m_cross,
    w_pair, w_out, w_recv, w_x, w_via, w_ring, w_final, w_turn,
    t_out, t_recv, t_mine, t_via, t_ring, t_cross,
    load, kv_send, kv_recv, og_send, og_recv,
    m_send, m_rsem, w_send, w_rsem, ws_send, ws_recv, wx_send, wx_recv, wf_sem,
    t_send, t_rsem, ts_send, ts_recv,
):
    s = lax.axis_index("seq")
    t = lax.axis_index("tp")
    y, x, c = s // 4, (s // 2) % 2, s % 2
    xh, z = t // 4, t % 4

    def slot(ys, xs, cs):
        return (ys * 2 + xs) * 2 + cs

    y_plus = {"seq": slot((y + 1) % 4, x, c)}
    y_minus = {"seq": slot((y + 3) % 4, x, c)}
    x_near = {"seq": slot(y, 1 - x, c)}
    sibling = {"seq": slot(y, x, 1 - c)}
    z_plus = {"tp": xh * 4 + (z + 1) % 4}
    z_minus = {"tp": xh * 4 + (z + 3) % 4}
    x_far = {"tp": (1 - xh) * 4 + z}

    barrier = pltpu.get_barrier_semaphore()
    partners = (y_plus, y_minus, x_near, sibling, z_plus, z_minus, x_far)
    for partner in partners:
        pl.semaphore_signal(barrier, inc=1, device_id=partner, device_id_type=MESH)

    loads = [
        pltpu.make_async_copy(src, dst, load.at[n])
        for n, (src, dst) in enumerate(
            (
                (k_ref.at[0], kv.at[s, 0, pl.ds(0, ROWS)]),
                (v_ref.at[0], kv.at[s, 1, pl.ds(0, ROWS)]),
                (og_ref, og.at[t]),
                (k_ref.at[1], noisy_kv.at[0]),
                (v_ref.at[1], noisy_kv.at[1]),
                (weight_ref, w_ref),
                (q_in, q_ref),
            )
        )
    ]
    for copy in loads[:3]:
        copy.start()

    mark_row = lax.broadcasted_iota(jnp.int32, (POS_ROWS, INNER_DEV), 0)
    lane = lax.broadcasted_iota(jnp.int32, (8, BOTH), 1)
    lane_block = (lane % ROWS) // BLOCK
    marks = jnp.zeros((POS_ROWS, INNER_DEV), F32)
    start = jnp.zeros((8, BOTH), F32)
    for b in range(POS_ROWS):
        position = order_ref[b].astype(F32)
        marks = jnp.where(mark_row == b, position, marks)
        start = jnp.where(lane_block == b, position * float(BLOCK), start)
    kv[s, 0, ROWS:] = marks.astype(BF16)
    limit[...] = start + jnp.where(lane < ROWS, lane % BLOCK, -1).astype(F32)

    def kv_copy(place, half, sem, device):
        part = kv.at[place, half, pl.ds(0, ROWS if half else ROWS + POS_ROWS)]
        return remote(part, part, kv_send.at[sem], kv_recv.at[place, half], device)

    near_place = slot(y, 1 - x, c)

    def ring_place(p, off):
        return slot((y + off) % 4, (x + p) % 2, c)

    def own_copy(kind, half):
        at = {"sibling": 0, "x": 16, "plus": 18, "minus": 20}[kind] + half
        device = {"sibling": sibling, "x": x_near, "plus": y_plus, "minus": y_minus}[kind]
        return kv_copy(s, half, at, device)

    def near_copy(kind, half):
        at = {"plus": 22, "minus": 24}[kind] + half
        return kv_copy(near_place, half, at, {"plus": y_plus, "minus": y_minus}[kind])

    def pass_plus(p):
        return kv_copy(ring_place(p, 3), 0, 26 + 2 * p, y_plus)

    def pass_minus(p):
        return kv_copy(ring_place(p, 1), 1, 27 + 2 * p, y_minus)

    def og_copy(place, half, sem, device, part=None):
        rows = {None: pl.ds(0, ROWS), 0: pl.ds(0, SPLIT), 1: pl.ds(SPLIT, ROWS - SPLIT)}[part]
        piece = og.at[place, half, rows]
        recv = og_recv.at[place, half + (2 if part == 1 else 0)]
        return remote(piece, piece, og_send.at[sem], recv, device)

    far_place = (1 - xh) * 4 + z

    def og_own(kind, half):
        if kind == "far":
            return og_copy(t, half, half, x_far, 0)
        at = {"plus": 2, "minus": 4}[kind] + half
        return og_copy(t, half, at, {"plus": z_plus, "minus": z_minus}[kind])

    def og_far(kind, half):
        at = {"plus": 6, "minus": 8}[kind] + half
        return og_copy(far_place, half, at, {"plus": z_plus, "minus": z_minus}[kind], 0)

    def og_place(a, off):
        return ((xh + a) % 2) * 4 + (z + off) % 4

    def og_pass_plus(a):
        return og_copy(og_place(a, 3), 0, 10 + 2 * a, z_plus, 0 if a else None)

    def og_pass_minus(a):
        return og_copy(og_place(a, 1), 1, 11 + 2 * a, z_minus, 0 if a else None)

    def og_late(off, half):
        return og_copy(og_place(0, off), half, 14 + 2 * off + half, x_far, 1)

    def og_wait(place, halves=(0, 1), part=None):
        for half in halves:
            og_copy(place, half, 0, z_plus, part).wait_recv()

    loads[0].wait()
    loads[1].wait()
    pl.semaphore_wait(barrier, len(partners))
    for n in (0, 1):
        own_copy("x", n).start()
        own_copy("plus", n).start()
        own_copy("minus", 1 - n).start()
    loads[2].wait()
    for n in (0, 1):
        og_own("plus", n).start()
        og_own("minus", 1 - n).start()
        og_own("far", n).start()
        own_copy("sibling", n).start()
    for n in (0, 1):
        og_late(0, n).start()
    for n in (6, 3, 4, 5):
        loads[n].start()
    loads[6].wait()

    for h in range(HEADS_DEV):
        cols = slice(h * HEAD_SIZE, (h + 1) * HEAD_SIZE)
        scaled = q_ref[:, cols].astype(F32).T * LOG2_SCALE
        high = scaled.astype(BF16)
        qt[h, :HEAD_SIZE] = high
        qt[h, HEAD_SIZE:] = (scaled - high.astype(F32)).astype(BF16)

    def cols_of(h):
        return slice(h * HEAD_SIZE, (h + 1) * HEAD_SIZE)

    def scores_of(key, h, first):
        return dot(jnp.concatenate([key, key], axis=1), qt[h, :, first:])

    loads[3].wait()
    loads[4].wait()
    row_block = lax.broadcasted_iota(jnp.int32, (ROWS, ROWS), 0) // BLOCK
    col_block = lax.broadcasted_iota(jnp.int32, (ROWS, ROWS), 1) // BLOCK
    self_bias = jnp.where(row_block == col_block, 0.0, MASKED).astype(F32)
    bias[:, :ROWS] = self_bias

    for h in range(HEADS_DEV):
        scores = scores_of(noisy_kv[0, :, cols_of(h)], h, ROWS) + bias[:, :ROWS]
        top = jnp.max(scores, axis=0, keepdims=True)
        weights = jnp.exp2(scores - top)
        stat[0, h : h + 1, :ROWS] = jnp.full((1, ROWS), LOWEST, F32)
        stat[0, h : h + 1, ROWS:] = top
        stat[1, h : h + 1, :ROWS] = jnp.zeros((1, ROWS), F32)
        stat[1, h : h + 1, ROWS:] = jnp.sum(weights, axis=0, keepdims=True)
        acc[cols_of(h), :ROWS] = jnp.zeros((HEAD_SIZE, ROWS), F32)
        acc[cols_of(h), ROWS:] = dot_tn(noisy_kv[1, :, cols_of(h)], weights.astype(BF16))

    def set_bias(place):
        position = kv[place, 0, ROWS:, :HEAD_SIZE].astype(F32)
        offset = lax.broadcasted_iota(jnp.int32, (BLOCK, HEAD_SIZE), 0).astype(F32)
        for b in range(POS_ROWS):
            code = position[b : b + 1] * float(BLOCK) + offset
            for n in range(BOTH // HEAD_SIZE):
                lanes = slice(n * HEAD_SIZE, (n + 1) * HEAD_SIZE)
                bias[b * BLOCK : (b + 1) * BLOCK, lanes] = jnp.where(
                    code <= limit[0:1, lanes], 0.0, MASKED
                ).astype(F32)

    def columns(j):
        return pl.ds(pl.multiple_of(j * WIDTH, HEAD_SIZE), WIDTH)

    half_rows = INNER_DEV // 2
    head_t[...] = jnp.zeros((INNER_DEV, BOTH), F32)

    loads[5].wait()

    og_order = ((0, 0), (0, 3), (0, 1), (1, 0), (0, 2), (1, 3), (1, 1), (1, 2))

    def og_at(k):
        a = sum(u[0] * equal(k, n) for n, u in enumerate(og_order))
        off = sum(u[1] * equal(k, n) for n, u in enumerate(og_order))
        return og_place(a, off)

    def head_step(k, carry):
        j = og_at(k)
        head_t[...] += dot_nt(w_ref[:, columns(j)], og[j].reshape(BOTH, WIDTH))
        return carry

    def forward_step(i, carry):
        n, d = i // 2, i % 2
        p = n // 5 + (n + 6) // 7 - (n + 5) // 7
        m = (n + 1) % 3
        off = ((n + 6) // 8) * (m + 3 * ((2 - m) // 2))
        place = slot((y + off) % 4, (x + p) % 2, (c + d) % 2)

        @pl.when(i == 6)
        def _():
            og_wait(og_place(0, 3), (0,))
            og_pass_plus(0).start()
            og_wait(og_place(0, 1), (1,))
            og_pass_minus(0).start()

        @pl.when(i == 8)
        def _():
            og_wait(far_place, (0,), 0)
            og_far("plus", 0).start()
            og_wait(og_place(0, 3), (1,))
            og_wait(og_place(0, 1), (0,))
            for off in (3, 1):
                for half in (0, 1):
                    og_late(off, half).start()

        @pl.when(i == 12)
        def _():
            og_wait(og_place(0, 2))
            for half in (0, 1):
                og_late(2, half).start()

        @pl.when(i == 10)
        def _():
            og_wait(far_place, (1,), 0)
            og_far("minus", 1).start()
            og_far("plus", 1).start()
            og_far("minus", 0).start()

        @pl.when(i == 14)
        def _():
            og_wait(far_place, (0, 1), 1)
            lax.fori_loop(0, 5, head_step, 0)

        for half in (0, 1):

            @pl.when(i > 0)
            def _():
                kv_copy(place, half, 0, sibling).wait_recv()

            @pl.when(i == 2)
            def _():
                near_copy("plus", half).start()
                near_copy("minus", half).start()

            for side, at in ((0, 4), (1, 10)):

                @pl.when(i == at + 2 * half)
                def _():
                    (pass_minus if half else pass_plus)(side).start()

            @pl.when((i > 0) & (d == 0))
            def _():
                kv_copy(place, half, 2 * n + half, sibling).start()

        set_bias(place)
        for h in range(HEADS_DEV):
            scores = scores_of(kv[place, 0, :ROWS, cols_of(h)], h, 0) + bias[...]
            old = stat[0, h : h + 1]
            top = jnp.maximum(old, jnp.max(scores, axis=0, keepdims=True))
            weights = jnp.exp2(scores - top)
            factor = jnp.exp2(old - top)
            stat[0, h : h + 1] = top
            stat[1, h : h + 1] = stat[1, h : h + 1] * factor + jnp.sum(
                weights, axis=0, keepdims=True
            )
            acc[cols_of(h)] = acc[cols_of(h)] * factor + dot_tn(
                kv[place, 1, :ROWS, cols_of(h)], weights.astype(BF16)
            )
        return carry

    lax.fori_loop(0, 16, forward_step, 0)
    og_wait(og_place(1, 3), (0,), 0)
    og_pass_plus(1).start()
    og_wait(og_place(1, 1), (1,), 0)
    og_pass_minus(1).start()

    for h in range(HEADS_DEV):
        total = stat[1, h : h + 1]
        out = acc[cols_of(h)] / total
        att_t[cols_of(h)] = out.astype(BF16)
        att[:, cols_of(h)] = out.T.astype(BF16)
        stat[0, h : h + 1] = stat[0, h : h + 1] + jnp.log2(total)

    def mix_step(side, n, carry):
        j = side * 4 + n
        mixp[j] = dot(att[...], w_ref[:, columns(j)]).astype(BF16).reshape(2, ROWS, WIDTH)
        return carry

    def w_copy(j):
        return remote(w_out.at[j], w_recv.at[j], ws_send.at[j], ws_recv.at[j], sibling)

    def w_across(n):
        return remote(w_pair.at[2 * n + 1 - x], w_x.at[n], wx_send.at[n], wx_recv.at[n], x_near)

    def w_sum(j):
        w_copy(j).wait_recv()
        w_pair[j] = (w_pair[j].astype(F32) + w_recv[j].astype(F32)).astype(BF16)

        @pl.when(j % 2 == 1 - x)
        def _():
            w_across(j // 2).start()

    def projection_step(k, carry):
        j = og_at(k)

        for half, pieces in enumerate(((6, 7), (5, 7))):
            for n in pieces:

                @pl.when(k == n)
                def _():
                    og_wait(j, (half,), 0)

        @pl.when(k > 4)
        def _():
            og_wait(j, (0, 1), 1)
            head_step(k, 0)

        grads = og[j].reshape(BOTH, WIDTH)
        theirs = att_t[pl.ds(pl.multiple_of((1 - c) * half_rows, 16), half_rows)]
        w_out[j] = dot(theirs, grads).astype(BF16).reshape(2, half_rows // 2, WIDTH)
        w_copy(j).start()
        mine = att_t[pl.ds(pl.multiple_of(c * half_rows, 16), half_rows)]
        w_pair[j] = dot(mine, grads).astype(BF16).reshape(2, half_rows // 2, WIDTH)

        @pl.when(k > 0)
        def _():
            w_sum(og_at(k - 1))

        return carry

    half_stream = ROWS // 2
    mix_a, mix_b = (
        RingReduce(
            lambda p, r, first=n * half_stream: mixp.at[
                og_place(p, r), :, pl.ds(first, half_stream)
            ],
            m_via.at[n], m_ring.at[n], m_cross.at[n], m_send.at[n], m_rsem.at[n],
            z_plus, z_minus, x_far,
        )
        for n in (0, 1)
    )
    weight = RingReduce(
        lambda p, r: w_pair.at[((y + r) % 4) * 2 + (x + p) % 2], w_via, w_ring, None,
        w_send, w_rsem, y_plus, y_minus, x_near,
    )
    lax.fori_loop(0, 5, projection_step, 0)
    lax.fori_loop(0, 4, functools.partial(mix_step, 1 - xh), 0)
    mix_a.start("far", 1)
    mix_a.start("near", 1)
    mix_b.start("far", 1)
    lax.fori_loop(5, 7, projection_step, 0)
    lax.fori_loop(0, 4, functools.partial(mix_step, xh), 0)
    lax.fori_loop(7, 8, projection_step, 0)
    w_sum(og_at(7))

    turns = [(1, 2), (0, 2), (1, 1), (1, 3), (1, 0), (0, 1), (0, 3), (0, 0)]
    term = RingReduce(
        lambda p, r: t_recv.at[turns.index((p, r))], t_via, t_ring, t_cross,
        t_send, t_rsem, y_plus, y_minus, x_near,
    )

    for h in range(HEADS_DEV):
        grad = head_t[cols_of(h)]
        rounded = grad.astype(BF16)
        head[:, cols_of(h)] = grad.T.astype(BF16)
        stat[1, h : h + 1] = jnp.sum(
            rounded.astype(F32) * att_t[cols_of(h)].astype(F32), axis=0, keepdims=True
        )
        att_t[cols_of(h)] = rounded
        dq[cols_of(h)] = jnp.zeros((HEAD_SIZE, BOTH), F32)
    head_tb = att_t

    def backward_tile(key, value, h, first, masks):
        scores = scores_of(key, h, first) + masks
        probs = jnp.exp2(scores - stat[0, h : h + 1, first:])
        value_term = dot(probs.astype(BF16), head[first:, cols_of(h)])
        prob_grad = dot(value, head_tb[cols_of(h), first:])
        score_grad = (probs * (prob_grad - stat[1, h : h + 1, first:])).astype(BF16)
        key_term = dot(score_grad, q_ref[first:, cols_of(h)]) * SCALE
        dq[cols_of(h), first:] += dot_tn(key, score_grad)
        return key_term.astype(BF16), value_term.astype(BF16)

    def t_copy(j):
        return remote(t_out.at[j], t_recv.at[j], ts_send.at[j], ts_recv.at[j], sibling)

    w_mine = pl.multiple_of(c * half_rows, 16)

    def final_copy():
        part = w_final.at[pl.ds(w_mine, half_rows)]
        return remote(part, part, wf_sem.at[0], wf_sem.at[1], sibling)

    def backward_step(i, carry):
        odd, last, second = i % 2, equal(i, 15), equal(i, 1)
        late = (i + 13) // 16
        d = 1 - ((1 - odd) * late + last + second)
        j = late * (odd * ((i + 1) // 2) + (1 - odd) * (i // 2 - 1) - last) + equal(i, 2)
        p = sum(turn[0] * equal(j, n) for n, turn in enumerate(turns))
        off = sum(turn[1] * equal(j, n) for n, turn in enumerate(turns))
        place = slot((y + off) % 4, (x + p) % 2, (c + d) % 2)

        @pl.when(i == 1)
        def _():
            mix_a.join(1)
            mix_b.start("near", 1)

        @pl.when(i == 6)
        def _():
            mix_b.join(1)
            for part in (mix_a, mix_b):
                part.start("far", 0)
            for part in (mix_a, mix_b):
                part.start("near", 0)

        @pl.when(i == 8)
        def _():
            mix_a.to_partner()

        @pl.when(i == 9)
        def _():
            for n in range(4):
                w_across(n).wait_recv()
                mine = w_pair.at[2 * n + x]
                mine[...] = (mine[...].astype(F32) + w_x[n].astype(F32)).astype(BF16)
            weight.start("far", 0)
            weight.start("near", 0)

        @pl.when(i == 12)
        def _():
            mix_b.to_partner()

        @pl.when(i == 15)
        def _():
            weight.join(0)
            term.join(0)
            term.to_partner()

        set_bias(place)
        for h in range(HEADS_DEV):
            key_term, value_term = backward_tile(
                kv[place, 0, :ROWS, cols_of(h)], kv[place, 1, :ROWS, cols_of(h)], h, 0, bias[...]
            )
            t_mine[0, :, cols_of(h)] = key_term
            t_mine[1, :, cols_of(h)] = value_term

        @pl.when(d == 1)
        def _():
            t_out[j] = t_mine[...]
            t_copy(j).start()

        @pl.when(d == 0)
        def _():
            t_copy(j).wait_recv()
            t_recv[j] = (t_recv[j].astype(F32) + t_mine[...].astype(F32)).astype(BF16)

        for n, (p_now, r) in enumerate(turns):
            if r == 0:
                continue

            @pl.when(i == (2 * n + 2 if n else 1))
            def _():
                if r == 2:
                    term.start("far", p_now)
                else:
                    which = (0,) if r == 1 else (1,)
                    term.start("near", p_now, which)
                    if p_now == 1:
                        term.join(p_now, which)

        return carry

    lax.fori_loop(0, 16, backward_step, 0)

    mix_a.join(0)
    mix_b.join(0)
    bias[:, :ROWS] = self_bias
    for h in range(HEADS_DEV):
        key_term, value_term = backward_tile(
            noisy_kv[0, :, cols_of(h)], noisy_kv[1, :, cols_of(h)], h, ROWS, bias[:, :ROWS]
        )
        kg_ref[1, :, cols_of(h)] = key_term
        vg_ref[1, :, cols_of(h)] = value_term

    for h in range(HEADS_DEV):
        qg_ref[:, cols_of(h)] = (dq[cols_of(h)] * SCALE).T.astype(BF16)


    w_final[pl.ds(w_mine, half_rows)] = weight.gathered(0).reshape(half_rows, WIDTH)
    final_copy().start()
    w_theirs = pl.multiple_of((1 - c) * half_rows, 16)
    part = w_final.at[pl.ds(w_theirs, half_rows)]
    remote(part, part, wf_sem.at[0], wf_sem.at[1], sibling).wait_recv()
    for n in range(INNER_DEV // HEAD_SIZE):
        w_turn[:, cols_of(n)] = w_final[cols_of(n)].T
    wg_ref[...] = w_turn[pl.ds(pl.multiple_of(c * (WIDTH // 2), 8), WIDTH // 2)]

    terms = term.result().astype(BF16)
    kg_ref[0] = terms[0]
    vg_ref[0] = terms[1]
    mixed_ref[:, :half_stream] = mix_a.result().astype(BF16)
    mixed_ref[:, half_stream:] = mix_b.result().astype(BF16)

    for half in (0, 1):
        for kind in ("x", "plus", "minus"):
            own_copy(kind, half).wait_send()
        for kind in ("plus", "minus"):
            near_copy(kind, half).wait_send()
            og_own(kind, half).wait_send()
            og_far(kind, half).wait_send()
        for off in range(4):
            og_late(off, half).wait_send()
        og_own("far", half).wait_send()
        for n in range(8):
            kv_copy(s, half, 2 * n + half, sibling).wait_send()
    for n in range(8):
        w_copy(n).wait_send()
        t_copy(n).wait_send()
    for n in range(4):
        w_across(n).wait_send()
    for p in (0, 1):
        pass_plus(p).wait_send()
        pass_minus(p).wait_send()
        og_pass_plus(p).wait_send()
        og_pass_minus(p).wait_send()
    mix_a.finish()
    mix_b.finish()
    weight.finish((0,))
    term.finish()
    final_copy().wait_send()


def results_kernel(*refs):
    count = len(refs) // 2
    copies = [
        pltpu.make_async_copy(refs[n], refs[count + n], refs[-1].at[n]) for n in range(count)
    ]
    for copy in copies:
        copy.start()
    for copy in copies:
        copy.wait()


def local(queries, keys, values, block_order, out_weight, out_grad):
    unit = (2, ROWS, INNER_DEV)
    w_unit = (2, INNER_DEV // 4, WIDTH)
    m_unit = (2, ROWS, WIDTH)

    def buffer(*shape, dtype=BF16):
        return pltpu.VMEM(shape, dtype)

    def sums(u, *parts):
        return [buffer(*parts, 2, *u), buffer(*parts, 2, 2, *u), buffer(*parts, *u)]

    scratch = [
        buffer(16, 2, ROWS + POS_ROWS, INNER_DEV),
        buffer(*unit),
        buffer(*out_weight.shape),
        buffer(BOTH, INNER_DEV),
        buffer(8, *m_unit),
        buffer(8, BOTH, dtype=F32),
        buffer(HEADS_DEV, 2 * HEAD_SIZE, BOTH),
        buffer(INNER_DEV, BOTH, dtype=F32),
        buffer(2, 8, BOTH, dtype=F32),
        buffer(INNER_DEV, BOTH),
        buffer(BOTH, INNER_DEV),
        buffer(ROWS, BOTH, dtype=F32),
        buffer(INNER_DEV, BOTH, dtype=F32),
        buffer(BOTH, INNER_DEV),
        buffer(INNER_DEV, BOTH, dtype=F32),
        buffer(8, *m_unit), *sums((2, ROWS // 2, WIDTH), 2),
        buffer(8, *w_unit), buffer(8, *w_unit), buffer(8, *w_unit), buffer(4, *w_unit),
        *sums(w_unit)[:2], buffer(INNER_DEV, WIDTH, dtype=F32),
        buffer(WIDTH, INNER_DEV, dtype=F32),
        buffer(8, *unit), buffer(8, *unit), buffer(*unit), *sums(unit),
        *(
            pltpu.SemaphoreType.DMA(shape)
            for shape in (
                (7,), (30,), (16, 2), (22,), (8, 4), (2, 13), (2, 13), (13,), (13,),
                (8,), (8,), (4,), (4,), (2,), (13,), (13,), (8,), (8,),
            )
        ),
    ]
    whole = pl.BlockSpec(memory_space=pltpu.VMEM)
    anywhere = pl.BlockSpec(memory_space=pl.ANY)
    shapes = (
        jax.ShapeDtypeStruct(m_unit, BF16),
        jax.ShapeDtypeStruct((BOTH, INNER_DEV), BF16),
        jax.ShapeDtypeStruct(unit, BF16),
        jax.ShapeDtypeStruct(unit, BF16),
        jax.ShapeDtypeStruct((WIDTH // 2, INNER_DEV), F32),
    )
    results = pl.pallas_call(
        layer_kernel,
        out_shape=tuple(pltpu.VMEM(a.shape, a.dtype) for a in shapes),
        in_specs=[pl.BlockSpec(memory_space=pltpu.SMEM)] + [anywhere] * 5,
        out_specs=(whole,) * 5,
        scratch_shapes=scratch,
        compiler_params=pltpu.CompilerParams(
            collective_id=0, has_side_effects=True, vmem_limit_bytes=60 * 2**20
        ),
    )(block_order, queries.reshape(BOTH, INNER_DEV), keys, values, out_weight, out_grad)
    mixed, query_grad, key_grad, value_grad, weight_grad = pl.pallas_call(
        results_kernel,
        out_shape=shapes,
        in_specs=[whole] * 5,
        out_specs=(anywhere,) * 5,
        scratch_shapes=[pltpu.SemaphoreType.DMA((5,))],
    )(*(pltpu.with_memory_space_constraint(a, pltpu.VMEM) for a in results))
    return (mixed, query_grad.reshape(unit), key_grad, value_grad, weight_grad.T)


def solution(mesh):
    return jax.shard_map(
        local,
        mesh=mesh,
        in_specs=(
            P(None, "seq", "tp"),
            P(None, "seq", "tp"),
            P(None, "seq", "tp"),
            P("seq"),
            P("tp", None),
            P(None, "seq", "tp"),
        ),
        out_specs=(
            P(None, "seq", "tp"),
            P(None, "seq", "tp"),
            P(None, "seq", "tp"),
            P(None, "seq", "tp"),
            P("tp", "seq"),
        ),
        check_vma=False,
    )
```
